256 devices in a mesh: region: 64 (over y, z, core), pair: 4 (over x).
Axes of the slice: x: 4, y: 4, z: 8, core: 2. Of those that a mesh axis runs over, the one named last changes fastest.
Arguments:
- log_depth: float32 [4096, 768], P('region'), may hold values from -4 to 4
- cameras: float32 [4096, 8], P('region'), may hold values from -1 to 5.7, as said below
- pair_pose: float32 [48640, 8], P(('region', 'pair')), may hold values from -0.6 to 1.2, as said below
- depth_mean: float32 [4096, 768], P('region'), may hold values from -6 to 6
- depth_square: float32 [4096, 768], P('region'), may hold values from 1 to 30
- camera_mean: float32 [4096, 8], P('region'), may hold values from -192 to 192
- camera_square: float32 [4096, 8], P('region'), may hold values from 1000 to 30000
- pose_mean: float32 [48640, 8], P(('region', 'pair')), may hold values from -64 to 64
- pose_square: float32 [48640, 8], P(('region', 'pair')), may hold values from 100 to 3000
- pointmaps: bfloat16 [48640, 6, 768], P(('region', 'pair')), may hold values from -4 to 4
- confidence: bfloat16 [48640, 2, 768], P(('region', 'pair')), may hold values from 0.049804688 to 0.5
- pair_images: int32 [48640, 2], P(('region', 'pair')), may hold values from 0 to 4095, as said below
- pair_flag: int32 [48640], P(('region', 'pair')), may hold values from 0 to 1, as said below
Outputs:
- depth_next: float32 [4096, 768], P('region')
- camera_next: float32 [4096, 8], P('region')
- pose_next: float32 [48640, 8], P(('region', 'pair'))
- depth_mean_next: float32 [4096, 768], P(('region', 'pair'))
- depth_square_next: float32 [4096, 768], P(('region', 'pair'))
- camera_mean_next: float32 [4096, 8], P(('region', 'pair'))
- camera_square_next: float32 [4096, 8], P(('region', 'pair'))
- pose_mean_next: float32 [48640, 8], P(('region', 'pair'))
- pose_square_next: float32 [48640, 8], P(('region', 'pair'))
The draws below stay inside these ranges and needn't reach their ends.
Inputs may be any that keep to these rules, and one draw needn't show every extreme that they name: `pair_images`: rows are held 190 to a device, devices in order region-major. The first image of a row lies in the region of the device that holds it. A temporal row's second image is (first + k) mod 4096 with 1 <= k <= 4; a loop-closure row's second image lies in another region. On every device exactly 2 loop-closure rows name a second image in each region other than its own. `pair_flag`: marks which rows of pair_images are loop closures. `cameras`: columns 0 to 3 hold a quaternion whose first entry is 0.8 to 1.2 and whose others are -0.3 to 0.3, columns 4 to 6 a translation, column 7 a log focal length of 5.3 to 5.7. `pair_pose`: columns 0 to 3 hold a quaternion whose first entry is 0.8 to 1.2 and whose others are -0.3 to 0.3, columns 4 to 6 a translation, column 7 a log scale of -0.3 to 0.3.
All inputs are finite; a program needn't handle non-finite values.
Results may differ from the reference program's by a relative error of at most 0.0003.
Values sent between devices are 32-bit elements; how exact they have to be, the bound alone decides.
A program may use at most 128 MiB of HBM per device.

```python
import math
import jax
import jax.numpy as jnp
from jax import lax

ANCH_W = 32
ANCH_H = 24
ANCH = 768
IMG_DEV = 64
CAP = 2
NEIGHBOURS = 4
ITERS = 2
START = 300
LOOP_DEV = 126
TEMP_DEV = 64
PAIR_DEV = 190
IMG = 4096
PAIRS = 48640
N_REGION = 64
N_PAIR = 4


def pair_table(key):
    device_keys = jax.random.split(jax.random.fold_in(key, 11), N_REGION * N_PAIR)

    def one_device(device_key, device):
        region = device // N_PAIR
        lane = device % N_PAIR
        key_first, key_second, key_shuffle = jax.random.split(device_key, 3)
        local = lane + N_PAIR * jnp.arange(IMG_DEV // N_PAIR, dtype=jnp.int32)
        offsets = jnp.arange(1, NEIGHBOURS + 1, dtype=jnp.int32)
        temporal_first = (region * IMG_DEV + local)[:, None] + 0 * offsets[None, :]
        temporal_second = (temporal_first + offsets[None, :]) % IMG
        loop_rows = jnp.arange(LOOP_DEV, dtype=jnp.int32)
        target = (region + 1 + loop_rows // CAP) % N_REGION
        loop_first = region * IMG_DEV + jax.random.randint(key_first, (LOOP_DEV,), 0, IMG_DEV)
        loop_second = target * IMG_DEV + jax.random.randint(key_second, (LOOP_DEV,), 0, IMG_DEV)
        first = jnp.concatenate([temporal_first.reshape(-1), loop_first])
        second = jnp.concatenate([temporal_second.reshape(-1), loop_second])
        flags = jnp.concatenate([jnp.zeros((TEMP_DEV,), jnp.int32), jnp.ones((LOOP_DEV,), jnp.int32)])
        mixing = jax.random.permutation(key_shuffle, PAIR_DEV)
        return (jnp.stack([first[mixing], second[mixing]], 1), flags[mixing])
    table, flags = jax.vmap(one_device)(device_keys, jnp.arange(N_REGION * N_PAIR, dtype=jnp.int32))
    return (table.reshape(PAIRS, 2).astype(jnp.int32), flags.reshape(PAIRS).astype(jnp.int32))


def draw_pair_images(key, part):
    return pair_table(key)[0]


def draw_pair_flag(key, part):
    return pair_table(key)[1]


def quaternion_columns(key, count):
    key_lead, key_rest = jax.random.split(key)
    leading = jax.random.uniform(key_lead, (count, 1), jnp.float32, 0.8, 1.2)
    others = jax.random.uniform(key_rest, (count, 3), jnp.float32, -0.3, 0.3)
    return jnp.concatenate([leading, others], 1)


def draw_cameras(key, part):
    key = jax.random.fold_in(key, 3)
    key_rot, key_move, key_focal = jax.random.split(key, 3)
    turning = quaternion_columns(key_rot, IMG)
    moving = 0.5 * jax.random.truncated_normal(key_move, -2.0, 2.0, (IMG, 3), jnp.float32)
    focal_log = jax.random.uniform(key_focal, (IMG, 1), jnp.float32, 5.3, 5.7)
    return jnp.concatenate([turning, moving, focal_log], 1)


def draw_pair_pose(key, part):
    key = jax.random.fold_in(key, 5)
    key_rot, key_move, key_scale = jax.random.split(key, 3)
    turning = quaternion_columns(key_rot, PAIRS)
    moving = 0.3 * jax.random.truncated_normal(key_move, -2.0, 2.0, (PAIRS, 3), jnp.float32)
    scale_log = jax.random.uniform(key_scale, (PAIRS, 1), jnp.float32, -0.3, 0.3)
    return jnp.concatenate([turning, moving, scale_log], 1)


def level_of(rng, dims, pieces, smallest, largest):
    loudness, own = 1.0, jax.random.fold_in(rng, 6)
    for position, shards_of in pieces:
        steps = jnp.exp(jax.random.uniform(jax.random.fold_in(own, position), (shards_of,), jnp.float32, smallest / len(pieces), largest / len(pieces)))
        loudness = loudness * jnp.repeat(steps, dims[position] // shards_of).reshape([-1 if axis == position else 1 for axis in range(len(dims))])
    return loudness


def bell_draw(own_key, extent, scale, limit, pieces=(), kind=jnp.bfloat16):
    entries = scale * jax.random.normal(own_key, extent, jnp.float32)
    if pieces:
        entries = entries * level_of(own_key, extent, pieces, -0.22, 0.18)
    return jnp.clip(entries, -limit, limit).astype(kind)


def setup_inputs(seed: int = 0) -> dict:
    keys = jax.random.split(jax.random.key(seed), 14)
    return {
        "log_depth": bell_draw(keys[0], (IMG, ANCH), 0.3, 4.0, ((0, 64),), jnp.float32),
        "cameras": draw_cameras(jax.random.fold_in(keys[13], 71), 0),
        "pair_pose": draw_pair_pose(jax.random.fold_in(keys[13], 71), 0),
        "depth_mean": bell_draw(keys[3], (IMG, ANCH), 1.0, 6.0, ((0, 64),), jnp.float32),
        "depth_square": jnp.clip(jnp.exp(math.log(30.0) - 3.4011974 * jax.random.uniform(keys[4], (IMG, ANCH), jnp.float32) ** level_of(keys[4], (IMG, ANCH), ((0, 64),), -0.2, 0.2)), 1.0, 30.0),
        "camera_mean": bell_draw(keys[5], (IMG, 8), 30.0, 192.0, ((0, 64),), jnp.float32),
        "camera_square": jnp.clip(jnp.exp(math.log(30000.0) - 3.4011974 * jax.random.uniform(keys[6], (IMG, 8), jnp.float32) ** level_of(keys[6], (IMG, 8), ((0, 64),), -0.2, 0.2)), 1000.0, 30000.0),
        "pose_mean": bell_draw(keys[7], (PAIRS, 8), 10.0, 64.0, ((0, 256),), jnp.float32),
        "pose_square": jnp.clip(jnp.exp(math.log(3000.0) - 3.4011974 * jax.random.uniform(keys[8], (PAIRS, 8), jnp.float32) ** level_of(keys[8], (PAIRS, 8), ((0, 256),), -0.2, 0.2)), 100.0, 3000.0),
        "pointmaps": bell_draw(keys[9], (PAIRS, 6, ANCH), 1.0, 4.0, ((0, 256),)),
        "confidence": jnp.clip(jnp.exp(math.log(0.5) - 2.306499 * jax.random.uniform(keys[10], (PAIRS, 2, ANCH), jnp.float32) ** level_of(keys[10], (PAIRS, 2, ANCH), ((0, 256),), -0.2, 0.2)), 0.049804688, 0.5).astype(jnp.bfloat16),
        "pair_images": draw_pair_images(jax.random.fold_in(keys[13], 71), 0),
        "pair_flag": draw_pair_flag(jax.random.fold_in(keys[13], 71), 0),
    }


LEARN_RATE = 0.01
BETA_ONE = 0.9
BETA_TWO = 0.999
EPSILON = 1e-08

def rotation(quaternion):
    w = quaternion[..., 0]
    x = quaternion[..., 1]
    y = quaternion[..., 2]
    z = quaternion[..., 3]
    norm_sq = w * w + x * x + y * y + z * z
    matrix = [[w * w + x * x - y * y - z * z, 2.0 * (x * y - w * z), 2.0 * (x * z + w * y)], [2.0 * (x * y + w * z), w * w - x * x + y * y - z * z, 2.0 * (y * z - w * x)], [2.0 * (x * z - w * y), 2.0 * (y * z + w * x), w * w - x * x - y * y + z * z]]
    return [[entry / norm_sq for entry in line] for line in matrix]

def world_points(depth_log, camera):
    anchors = jnp.arange(ANCH, dtype=jnp.int32)
    across = (8 * (anchors % ANCH_W) + 4 - 4 * ANCH_W).astype(jnp.float32)
    downward = (8 * (anchors // ANCH_W) + 4 - 4 * ANCH_H).astype(jnp.float32)
    matrix = rotation(camera[:, 0:4])
    focal = jnp.exp(camera[:, 7:8])
    depth = jnp.exp(depth_log)
    local = [depth * across[None, :] / focal, depth * downward[None, :] / focal, depth]
    lines = []
    for axis_k in range(3):
        value = matrix[axis_k][0][:, None] * local[0] + matrix[axis_k][1][:, None] * local[1]
        value = value + matrix[axis_k][2][:, None] * local[2] + camera[:, 4 + axis_k][:, None]
        lines.append(value)
    return jnp.stack(lines, 1)

def pair_loss(chi_first, chi_second, pose, pointmaps, confidence, weight):
    matrix = rotation(pose[:, 0:4])
    scale = jnp.exp(pose[:, 7])[:, None, None]
    points = pointmaps.astype(jnp.float32).reshape(pose.shape[0], 2, 3, pointmaps.shape[2])
    placed = jnp.stack([chi_first, chi_second], 1)
    squares = jnp.zeros(confidence.shape, jnp.float32)
    for axis_k in range(3):
        moved = matrix[axis_k][0][:, None, None] * points[:, :, 0] + matrix[axis_k][1][:, None, None] * points[:, :, 1]
        moved = moved + matrix[axis_k][2][:, None, None] * points[:, :, 2] + pose[:, 4 + axis_k][:, None, None]
        gap = placed[:, :, axis_k] - scale * moved
        squares = squares + gap * gap
    return jnp.sum(weight[:, None, None] * confidence.astype(jnp.float32) * squares)

def pair_gradients(chi_first, chi_second, pose, pointmaps, confidence, weight):
    return jax.grad(pair_loss, argnums=(0, 1, 2))(chi_first, chi_second, pose, pointmaps, confidence, weight)

def adam_step(param, gradient, mean, square, step_count):
    mean = BETA_ONE * mean + (1.0 - BETA_ONE) * gradient
    square = BETA_TWO * square + (1.0 - BETA_TWO) * gradient * gradient
    fix_one = 1.0 - BETA_ONE ** step_count
    fix_two = 1.0 - BETA_TWO ** step_count
    param = param - LEARN_RATE * (mean / fix_one) / (jnp.sqrt(square / fix_two) + EPSILON)
    return (param, mean, square)

def reference(log_depth, cameras, pair_pose, depth_mean, depth_square, camera_mean, camera_square, pose_mean, pose_square, pointmaps, confidence, pair_images, pair_flag):
    weight = 1.0 + pair_flag.astype(jnp.float32)
    blocks = PAIRS // PAIR_DEV

    def split(array):
        return array.reshape((blocks, PAIR_DEV) + array.shape[1:])
    firsts = split(pair_images[:, 0].astype(jnp.int32))
    seconds = split(pair_images[:, 1].astype(jnp.int32))
    for step_index in range(ITERS):
        chi = world_points(log_depth, cameras)

        def visit(total, block):
            first, second, pose, points, conf, wts = block
            g_first, g_second, g_pose = pair_gradients(chi[first], chi[second], pose, points, conf, wts)
            total = total.at[first].add(g_first).at[second].add(g_second)
            return (total, g_pose)
        g_chi, g_pose = lax.scan(visit, jnp.zeros_like(chi), (firsts, seconds, split(pair_pose), split(pointmaps), split(confidence), split(weight)))
        unused, pull = jax.vjp(world_points, log_depth, cameras)
        g_depth, g_camera = pull(g_chi)
        step_count = START + step_index + 1
        log_depth, depth_mean, depth_square = adam_step(log_depth, g_depth, depth_mean, depth_square, step_count)
        cameras, camera_mean, camera_square = adam_step(cameras, g_camera, camera_mean, camera_square, step_count)
        pair_pose, pose_mean, pose_square = adam_step(pair_pose, g_pose.reshape(PAIRS, 8), pose_mean, pose_square, step_count)
    return (log_depth, cameras, pair_pose, depth_mean, depth_square, camera_mean, camera_square, pose_mean, pose_square)
```

```python
import functools

import jax
import jax.numpy as jnp
from jax import lax
from jax.experimental import pallas as pl
from jax.experimental.pallas import tpu as pltpu
from jax.sharding import PartitionSpec as P

ANCH_W = 32
ANCH_H = 24
ANCH = 768
CAP = 2
NEIGHBOURS = 4
ITERS = 2
START = 300

LEARN_RATE = 0.01
BETA_ONE = 0.9
BETA_TWO = 0.999
EPSILON = 1e-08

TILES = ANCH // 128
EDGE = 8
MSG = 16
F32 = jnp.float32
BF16 = jnp.bfloat16


def rounded(value, multiple):
    return -(-value // multiple) * multiple


def split_two(x):
    high = x.astype(BF16)
    return high, (x - high.astype(F32)).astype(BF16)


def split_three(x):
    high = x.astype(BF16)
    rest = x - high.astype(F32)
    middle = rest.astype(BF16)
    return high, middle, (rest - middle.astype(F32)).astype(BF16)


def dot(a, b):
    return jnp.dot(a, b, preferred_element_type=F32)


def dot_exact(one_hot, x):
    high, middle, low = split_three(x)
    return dot(one_hot, high) + (dot(one_hot, middle) + dot(one_hot, low))


def rotation_rows(w, x, y, z):
    inverse = 1.0 / (w * w + x * x + y * y + z * z)
    matrix = [
        [w * w + x * x - y * y - z * z, 2.0 * (x * y - w * z), 2.0 * (x * z + w * y)],
        [2.0 * (x * y + w * z), w * w - x * x + y * y - z * z, 2.0 * (y * z - w * x)],
        [2.0 * (x * z - w * y), 2.0 * (y * z + w * x), w * w - x * x - y * y + z * z],
    ]
    return [[entry * inverse for entry in line] for line in matrix], inverse


def rotation_pull(q, matrix, inverse, g):
    w, x, y, z = q
    along = sum(g[k][j] * matrix[k][j] for k in range(3) for j in range(3))
    diag = g[0][0] + g[1][1] + g[2][2]
    g_w = w * diag + z * (g[1][0] - g[0][1]) + y * (g[0][2] - g[2][0]) + x * (g[2][1] - g[1][2])
    g_x = (
        x * (g[0][0] - g[1][1] - g[2][2])
        + y * (g[0][1] + g[1][0])
        + z * (g[0][2] + g[2][0])
        + w * (g[2][1] - g[1][2])
    )
    g_y = (
        y * (g[1][1] - g[0][0] - g[2][2])
        + x * (g[0][1] + g[1][0])
        + z * (g[1][2] + g[2][1])
        + w * (g[0][2] - g[2][0])
    )
    g_z = (
        z * (g[2][2] - g[0][0] - g[1][1])
        + x * (g[0][2] + g[2][0])
        + y * (g[1][2] + g[2][1])
        + w * (g[1][0] - g[0][1])
    )
    twice = 2.0 * inverse
    return [twice * (g_w - w * along), twice * (g_x - x * along), twice * (g_y - y * along), twice * (g_z - z * along)]


def adam(param, gradient, mean, square, first):
    fixes = [(1.0 - BETA_ONE ** (START + 1 + i), 1.0 - BETA_TWO ** (START + 1 + i)) for i in range(ITERS)]
    fix_one = jnp.where(first, F32(fixes[0][0]), F32(fixes[1][0]))
    fix_two = jnp.where(first, F32(fixes[0][1]), F32(fixes[1][1]))
    mean = BETA_ONE * mean + (1.0 - BETA_ONE) * gradient
    square = BETA_TWO * square + (1.0 - BETA_TWO) * gradient * gradient
    param = param - LEARN_RATE * (mean / fix_one) / (jnp.sqrt(square / fix_two) + EPSILON)
    return param, mean, square


def kernel(
    regions, lanes, own, pairs,
    logd_in, cam_in, pose_in, dmean_in, dsq_in, cmean_in, csq_in, pmean_in, psq_in, points_in, conf_in, images_in, flag_in,
    logd_out, cam_out, pose_out, dmean_out, dsq_out, cmean_out, csq_out, pmean_out, psq_out,
    logd, dmean, dsq, cam, cmean, csq, pose, pmean, psq, points, conf, xs, cw,
    index_rows, gather_hot, scatter_hot, answer_hot, return_hot,
    table, small_table, rows_d, rows_c, rows_g, rows_s, pair_s, wide, narrow, grad_d,
    req_out, req_in, ans_out, ans_in, ret_out, ret_in, edge_d, edge_c, back_d, back_c, part_d, part_c,
    load_sem, send_sem, recv_sem, small_send, small_recv,
):
    share = own // lanes
    slots = CAP * regions
    pair_rows = xs.shape[1]
    pair_lanes = pose.shape[1]
    keys = table.shape[1]
    edge_at = own
    slot_at = own + 16
    region = lax.axis_index("region")
    lane = lax.axis_index("pair")
    my_rows = pl.multiple_of(lane * share, share)

    def ahead(j):
        return lax.rem(region + j, regions)

    def behind(j):
        return lax.rem(region - j + regions, regions)

    def lane_at(k):
        return lax.rem(lane + k, lanes)

    barrier = pltpu.get_barrier_semaphore()

    def greet(j, carry):
        pl.semaphore_signal(barrier, inc=1, device_id={"region": ahead(j)})
        return carry

    lax.fori_loop(1, regions, greet, 0)
    for k in range(1, lanes):
        pl.semaphore_signal(barrier, inc=1, device_id={"pair": lane_at(k)})

    loads = [
        pltpu.make_async_copy(points_in, points, load_sem.at[0]),
        pltpu.make_async_copy(conf_in, conf, load_sem.at[1]),
        pltpu.make_async_copy(dmean_in.at[pl.ds(my_rows, share)], dmean, load_sem.at[2]),
        pltpu.make_async_copy(dsq_in.at[pl.ds(my_rows, share)], dsq, load_sem.at[3]),
        pltpu.make_async_copy(logd_in, logd.at[0], load_sem.at[4]),
    ]
    for load in loads:
        load.start()

    lane_ids = lax.broadcasted_iota(jnp.int32, (1, pair_lanes), 1)
    index_rows[...] = jnp.zeros_like(index_rows)
    index_rows[0:1, 0:pairs] = images_in[0:1, :]
    index_rows[1:2, 0:pairs] = images_in[1:2, :]
    index_rows[2:3, 0:pairs] = flag_in[...]
    real = lane_ids < pairs
    seconds = index_rows[1:2, :]
    remote = jnp.logical_and(index_rows[2:3, :] == 1, real)
    firsts = jnp.where(real, index_rows[0:1, :] - region * own, 0)
    target = lax.div(seconds, jnp.full_like(seconds, own))
    local = seconds - target * own
    offset = target - region
    offset = jnp.where(offset < 0, offset + regions, offset)
    offset = jnp.where(remote, offset, 0)
    offset_column = jnp.transpose(jnp.broadcast_to(offset.astype(F32), (128, pair_lanes)))[:, 0:1]
    earlier_ids = lax.broadcasted_iota(jnp.int32, (pair_lanes, pair_lanes), 0)
    later_ids = lax.broadcasted_iota(jnp.int32, (pair_lanes, pair_lanes), 1)
    same = jnp.logical_and(offset_column == offset.astype(F32), earlier_ids < later_ids)
    rank = jnp.sum(jnp.where(same, 1.0, 0.0), axis=0, keepdims=True).astype(jnp.int32)
    slot = rank * regions + offset - 1
    slot = jnp.where(remote, slot, -1)
    near = jnp.where(target == region, local, edge_at + local)
    near = jnp.where(real, near, 0)
    second_row = jnp.where(remote, slot_at + slot, near)
    wanted = jnp.sum(
        jnp.where(lax.broadcasted_iota(jnp.int32, (slots, pair_lanes), 0) == slot, local.astype(F32), 0.0),
        axis=1,
        keepdims=True,
    )
    half = lax.broadcasted_iota(jnp.int32, (regions, 128), 1) < 64
    request = jnp.where(half, wanted[0:regions], wanted[regions:slots])
    req_out[...] = jnp.broadcast_to(request[:, None, :], req_out.shape)
    req_in[regions - 1] = jnp.full(req_in.shape[1:], -1.0, F32)

    pl.semaphore_wait(barrier, regions - 1 + lanes - 1)

    def ask(j, carry):
        pltpu.make_async_remote_copy(
            src_ref=req_out.at[j - 1],
            dst_ref=req_in.at[j - 1],
            send_sem=small_send.at[0],
            recv_sem=small_recv.at[0],
            device_id={"region": ahead(j)},
        ).start()
        return carry

    lax.fori_loop(1, regions, ask, 0)

    for s, row in enumerate((firsts, second_row)):
        column = jnp.transpose(jnp.broadcast_to(row.astype(F32), (128, pair_lanes)))[0:pair_rows, 0:1]
        key_ids = lax.broadcasted_iota(jnp.int32, (pair_rows, keys), 1).astype(F32)
        gather_hot[s] = jnp.where(column == key_ids, 1.0, 0.0).astype(BF16)
        row_ids = lax.broadcasted_iota(jnp.int32, (keys, pair_lanes), 0)
        scatter_hot[:, s * pair_lanes : (s + 1) * pair_lanes] = jnp.where(row_ids == row, 1.0, 0.0).astype(BF16)

    ones = jnp.ones((8, cam.shape[1]), F32)
    cam[...] = ones
    cmean[...] = ones
    csq[...] = ones
    cam[:, 0:own] = cam_in[...]
    cmean[:, 0:own] = cmean_in[...]
    csq[:, 0:own] = csq_in[...]
    ones = jnp.ones((8, pair_lanes), F32)
    pose[...] = ones
    pmean[...] = ones
    psq[...] = ones
    pose[:, 0:pairs] = pose_in[...]
    pmean[:, 0:pairs] = pmean_in[...]
    psq[:, 0:pairs] = psq_in[...]
    wide[...] = jnp.zeros_like(wide)
    narrow[...] = jnp.zeros_like(narrow)
    rows_g[...] = jnp.zeros_like(rows_g)
    rows_s[...] = jnp.zeros_like(rows_s)
    pair_s[...] = jnp.zeros_like(pair_s)
    table[...] = jnp.zeros_like(table)
    small_table[...] = jnp.zeros_like(small_table)
    loads[4].wait()
    loads[0].wait()
    loads[1].wait()

    weight_row = jnp.where(real, 2.0 * (1.0 + index_rows[2:3, :].astype(F32)), 0.0)
    weight = jnp.transpose(jnp.broadcast_to(weight_row, (128, pair_lanes)))[0:pairs, 0:1]

    def convert(c, carry):
        xs[c, 0:pairs, :] = points[c].astype(F32)
        return carry

    if pair_rows > pairs:
        xs[:, pair_rows - 8 : pair_rows, :] = jnp.zeros((6, 8, ANCH), F32)
        cw[:, pair_rows - 8 : pair_rows, :] = jnp.zeros((2, 8, ANCH), F32)
    lax.fori_loop(0, 6, convert, 0)
    for s in range(2):
        cw[s, 0:pairs, :] = conf[s].astype(F32) * weight

    anchor = lax.broadcasted_iota(jnp.int32, (8, 128), 1)
    across = (8 * lax.rem(anchor, jnp.full_like(anchor, ANCH_W)) + 4 - 4 * ANCH_W).astype(F32)
    downward = (8 * lax.div(anchor, jnp.full_like(anchor, ANCH_W)) + 4 - 4 * ANCH_H).astype(F32)
    down_step = 8.0 * (128 // ANCH_W)
    column_ids = lax.broadcasted_iota(jnp.int32, (8, 128), 1)

    def wait_small(sem, which, count):
        pltpu.make_async_copy(req_in.at[pl.ds(0, count)], req_in.at[pl.ds(0, count)], sem.at[which]).wait()

    def wait_messages(sem, which):
        whole = ans_in.at[0, pl.ds(0, MSG * (regions - 1))]
        pltpu.make_async_copy(whole, whole, sem.at[which]).wait()

    wait_small(small_recv, 0, regions - 1)
    asked = req_in[:, 0, :]
    ids = lax.broadcasted_iota(jnp.int32, (regions, own), 1).astype(F32)
    for c in range(CAP):
        hot = jnp.where(asked[:, 64 * c : 64 * c + 1] == ids, 1.0, 0.0)
        answer_hot[c * regions : (c + 1) * regions, :] = hot.astype(BF16)
    asked_rows = jnp.transpose(jnp.concatenate([asked, asked], 0)) if regions == 64 else None
    if regions == 64:
        both = jnp.concatenate([asked_rows[0:1, 0:64], asked_rows[64:65, 0:64]], 1)
        row_ids = lax.broadcasted_iota(jnp.int32, (own, slots), 0).astype(F32)
        return_hot[...] = jnp.where(row_ids == both, 1.0, 0.0).astype(BF16)
    else:
        return_hot[...] = jnp.transpose(answer_hot[...].astype(F32)).astype(BF16)

    def send_messages(it, phase, src, dst, towards):
        def send(j, carry):
            at = pl.ds(pl.multiple_of((j - 1) * MSG, MSG), MSG)
            pltpu.make_async_remote_copy(
                src_ref=src.at[it, at],
                dst_ref=dst.at[it, at],
                send_sem=send_sem.at[2 * it + phase],
                recv_sem=recv_sem.at[2 * it + phase],
                device_id={"region": towards(j)},
            ).start()
            return carry

        lax.fori_loop(1, regions, send, 0)

    def pack(dst, it, depths, smalls):
        for c in range(CAP):
            for g in range(regions // 8):
                rows = slice(c * regions + 8 * g, c * regions + 8 * g + 8)
                for t in range(TILES):
                    at = MSG * 8 * g + TILES * c + t
                    dst[it, pl.ds(at, 8, stride=MSG), :] = depths[rows, 128 * t : 128 * t + 128]
        for g in range(regions // 8):
            low = smalls[8 * g : 8 * g + 8, :]
            high = smalls[regions + 8 * g : regions + 8 * g + 8, :]
            dst[it, pl.ds(MSG * 8 * g + CAP * TILES, 8, stride=MSG), :] = low + pltpu.roll(high, 64, 1)

    def unpack_depths(src, it, c, g, t):
        return src[it, pl.ds(MSG * 8 * g + TILES * c + t, 8, stride=MSG), :]

    def unpack_smalls(src, it, c, g):
        value = src[it, pl.ds(MSG * 8 * g + CAP * TILES, 8, stride=MSG), :]
        value = jnp.where(column_ids < 64, value, 0.0) if c == 0 else jnp.where(column_ids < 64, pltpu.roll(value, 64, 1), 0.0)
        return value

    def small_copy(it, phase, src, dst, device_id):
        return pltpu.make_async_remote_copy(
            src_ref=src,
            dst_ref=dst,
            send_sem=small_send.at[1 + 16 * it + phase],
            recv_sem=small_recv.at[1 + 16 * it + phase],
            device_id=device_id,
        )

    def iteration(it, carry):
        first = it == 0
        q = [cam[k : k + 1, :] for k in range(4)]
        turn, turn_inverse = rotation_rows(*q)
        near_focal = jnp.exp(-cam[7:8, :])
        for k in range(3):
            narrow[4 * k : 4 * k + 1, :] = turn[k][0] * near_focal
            narrow[4 * k + 1 : 4 * k + 2, :] = turn[k][1] * near_focal
            narrow[4 * k + 2 : 4 * k + 3, :] = turn[k][2]
            narrow[4 * k + 3 : 4 * k + 4, :] = cam[4 + k : 5 + k, :]
        coefs = jnp.transpose(narrow[...])[0:own, :]
        small_table[0:own, :] = coefs
        depth = jnp.exp(logd[it])
        edge_d[it, 0] = depth[0:EDGE, :]
        edge_c[it, 0] = coefs[0:EDGE, :]
        edge_copies = [
            small_copy(it, 0, edge_d.at[it, 0], edge_d.at[it, 1], {"region": behind(1)}),
            small_copy(it, 1, edge_c.at[it, 0], edge_c.at[it, 1], {"region": behind(1)}),
        ]
        for copy in edge_copies:
            copy.start()
        pieces = split_three(depth)
        for n in range(3):
            table[n, 0:own, :] = pieces[n]
        answer = dot(answer_hot[...], pieces[0]) + (dot(answer_hot[...], pieces[1]) + dot(answer_hot[...], pieces[2]))
        pack(ans_out, it, answer, dot_exact(answer_hot[...], coefs))
        send_messages(it, 0, ans_out, ans_in, behind)

        p = [pose[k : k + 1, :] for k in range(4)]
        bend, bend_inverse = rotation_rows(*p)
        scale = jnp.exp(pose[7:8, :])
        for k in range(3):
            for j in range(3):
                wide[4 * k + j : 4 * k + j + 1, :] = scale * bend[k][j]
            wide[4 * k + 3 : 4 * k + 4, :] = scale * pose[4 + k : 5 + k, :]
        rows_p = jnp.transpose(wide[...])
        rows_s[1, 0:pair_lanes, :] = rows_p

        for copy in edge_copies:
            copy.wait_recv()
        pieces = split_three(jnp.concatenate([edge_d[it, 1], jnp.zeros((8, ANCH), F32)], 0))
        for n in range(3):
            table[n, edge_at : edge_at + 16, :] = pieces[n]
        small_table[edge_at : edge_at + EDGE, :] = edge_c[it, 1]
        wait_messages(recv_sem, 2 * it)
        ans_in[it, MSG * (regions - 1) : MSG * regions, :] = jnp.zeros((MSG, 128), F32)
        for c in range(CAP):
            for g in range(0, regions // 8, 2):
                at = slot_at + c * regions + 8 * g
                for t in range(TILES):
                    value = jnp.concatenate(
                        [unpack_depths(ans_in, it, c, g, t), unpack_depths(ans_in, it, c, g + 1, t)], 0
                    )
                    pieces = split_three(value)
                    for n in range(3):
                        table[n, at : at + 16, 128 * t : 128 * t + 128] = pieces[n]
                small_table[at : at + 8, :] = unpack_smalls(ans_in, it, c, g)
                small_table[at + 8 : at + 16, :] = unpack_smalls(ans_in, it, c, g + 1)

        for s in range(2):
            for n in range(0, ANCH, 256):
                part = slice(n, n + 256)
                rows_d[s, :, part] = dot(gather_hot[s], table[0, :, part]) + (
                    dot(gather_hot[s], table[1, :, part]) + dot(gather_hot[s], table[2, :, part])
                )
            rows_c[s] = dot_exact(gather_hot[s], small_table[...])

        def group(g, inner):
            at = pl.ds(pl.multiple_of(g * 8, 8), 8)
            pose_values = rows_s[1, at, :]

            def spread(values, c):
                return jnp.broadcast_to(values[:, c : c + 1], (8, 128))

            shift = [[spread(pose_values, 4 * k + j) for j in range(4)] for k in range(3)]
            turned = [[jnp.zeros((8, 128), F32) for j in range(3)] for k in range(3)]
            moved = [jnp.zeros((8, 128), F32) for k in range(3)]
            for s in range(2):
                camera = rows_c[s, at, :]
                ray = []
                step = []
                place = []
                for k in range(3):
                    down = spread(camera, 4 * k + 1)
                    ray.append(spread(camera, 4 * k) * across + (down * downward + spread(camera, 4 * k + 2)))
                    step.append(down * down_step)
                    place.append(spread(camera, 4 * k + 3))
                total = [jnp.zeros((8, 128), F32) for k in range(3)]
                by_depth = [jnp.zeros((8, 128), F32) for k in range(3)]
                by_down = [jnp.zeros((8, 128), F32) for k in range(3)]
                for t in range(TILES):
                    part = slice(128 * t, 128 * t + 128)
                    d = rows_d[s, at, part]
                    c = cw[s, at, part]
                    x = [xs[3 * s + j, at, part] for j in range(3)]
                    along = None
                    for k in range(3):
                        placed = shift[k][0] * x[0] + shift[k][1] * x[1] + (shift[k][2] * x[2] + shift[k][3])
                        pull = c * ((d * ray[k] + place[k]) - placed)
                        for j in range(3):
                            turned[k][j] = turned[k][j] + pull * x[j]
                        total[k] = total[k] + pull
                        deep = pull * d
                        by_depth[k] = by_depth[k] + deep
                        if t > 0:
                            by_down[k] = by_down[k] + F32(t) * deep
                        along = deep * ray[k] if along is None else along + deep * ray[k]
                        if t < TILES - 1:
                            ray[k] = ray[k] + step[k]
                    rows_g[pl.ds(pl.multiple_of(s * pair_lanes + g * 8, 8), 8), part] = along
                out = jnp.zeros((8, 128), F32)
                for k in range(3):
                    moved[k] = moved[k] + total[k]
                    values = [
                        by_depth[k] * across,
                        by_depth[k] * downward + by_down[k] * down_step,
                        by_depth[k],
                        total[k],
                    ]
                    for j in range(4):
                        out = jnp.where(column_ids == 4 * k + j, jnp.sum(values[j], axis=1, keepdims=True), out)
                rows_s[0, pl.ds(pl.multiple_of(s * pair_lanes + g * 8, 8), 8), :] = out
            out = jnp.zeros((8, 128), F32)
            for k in range(3):
                for j in range(3):
                    out = jnp.where(column_ids == 4 * k + j, jnp.sum(turned[k][j], axis=1, keepdims=True), out)
                out = jnp.where(column_ids == 4 * k + 3, jnp.sum(moved[k], axis=1, keepdims=True), out)
            pair_s[at, :] = out
            return inner

        lax.fori_loop(0, pair_rows // 8, group, 0)

        last = rounded(slot_at + slots, 16)
        hot = scatter_hot[0:last, :]
        for n in range(0, ANCH, 256):
            part = slice(n, n + 256)
            high, low = split_two(rows_g[:, part])
            grad_d[:, part] = dot(hot, high) + dot(hot, low)
        sums = dot_exact(hot, rows_s[0])
        pack(ret_out, it, grad_d[slot_at : slot_at + slots, :], sums[slot_at : slot_at + slots, :])
        send_messages(it, 1, ret_out, ret_in, ahead)
        back_d[it, 0] = grad_d[edge_at : edge_at + EDGE, :]
        back_c[it, 0] = sums[edge_at : edge_at + EDGE, :]
        back_copies = [
            small_copy(it, 2, back_d.at[it, 0], back_d.at[it, 1], {"region": ahead(1)}),
            small_copy(it, 3, back_c.at[it, 0], back_c.at[it, 1], {"region": ahead(1)}),
        ]
        for copy in back_copies:
            copy.start()

        found = jnp.transpose(pair_s[...])
        m = [[found[4 * k + j : 4 * k + j + 1, :] for j in range(3)] for k in range(3)]
        v = [found[4 * k + 3 : 4 * k + 4, :] for k in range(3)]
        g_turn = [[-(scale * m[k][j]) for j in range(3)] for k in range(3)]
        g_pose = rotation_pull(p, bend, bend_inverse, g_turn)
        g_scale = sum(bend[k][j] * g_turn[k][j] for k in range(3) for j in range(3))
        for k in range(3):
            g_move = -(scale * v[k])
            g_scale = g_scale + pose[4 + k : 5 + k, :] * g_move
            g_pose.append(g_move)
        g_pose.append(g_scale)
        for k in range(8):
            row = slice(k, k + 1)
            pose[row, :], pmean[row, :], psq[row, :] = adam(pose[row, :], g_pose[k], pmean[row, :], psq[row, :], first)

        wait_messages(recv_sem, 2 * it + 1)
        for copy in back_copies:
            copy.wait_recv()
        ret_in[it, MSG * (regions - 1) : MSG * regions, :] = jnp.zeros((MSG, 128), F32)
        hot = return_hot[...]
        for t in range(TILES):
            part = slice(128 * t, 128 * t + 128)
            value = jnp.concatenate(
                [unpack_depths(ret_in, it, c, g, t) for c in range(CAP) for g in range(regions // 8)], 0
            )
            high, low = split_two(value)
            grad_d[0:own, part] = grad_d[0:own, part] + (dot(hot, high) + dot(hot, low))
        grad_d[0:EDGE, :] = grad_d[0:EDGE, :] + back_d[it, 1]
        value = jnp.concatenate([unpack_smalls(ret_in, it, c, g) for c in range(CAP) for g in range(regions // 8)], 0)
        sums = sums[0:own, :] + dot_exact(hot, value)
        sums = jnp.concatenate([sums[0:EDGE, :] + back_c[it, 1], sums[EDGE:own, :]], 0)
        if own < 128:
            sums = jnp.concatenate([sums, jnp.zeros((128 - own, 128), F32)], 0)
        part_c[it, lane] = jnp.transpose(sums)[0:16, :]

        lane_copies = []
        for k in range(1, lanes):
            to = lane_at(k)
            rows = pl.ds(pl.multiple_of(to * share, share), share)
            lane_copies.append(small_copy(it, 4 + k, grad_d.at[rows], part_d.at[it, k - 1], {"pair": to}))
            lane_copies.append(small_copy(it, 7 + k, part_c.at[it, lane], part_c.at[it, lane], {"pair": to}))
        for copy in lane_copies:
            copy.start()
        for copy in lane_copies:
            copy.wait_recv()
        gradient = grad_d[pl.ds(my_rows, share), :]
        for k in range(1, lanes):
            gradient = gradient + part_d[it, k - 1]
        updated, dmean[...], dsq[...] = adam(logd[it, pl.ds(my_rows, share), :], gradient, dmean[...], dsq[...], first)
        logd[it + 1, pl.ds(my_rows, share), :] = updated
        mine = logd.at[it + 1, pl.ds(my_rows, share)]
        gathers = [small_copy(it, 10 + k, mine, mine, {"pair": lane_at(k)}) for k in range(1, lanes)]
        for copy in gathers:
            copy.start()

        found = part_c[it, 0]
        for k in range(1, lanes):
            found = found + part_c[it, k]
        across_sum = [found[4 * k : 4 * k + 1, :] * near_focal for k in range(3)]
        down_sum = [found[4 * k + 1 : 4 * k + 2, :] * near_focal for k in range(3)]
        g_turn = [[across_sum[k], down_sum[k], found[4 * k + 2 : 4 * k + 3, :]] for k in range(3)]
        g_cam = rotation_pull(q, turn, turn_inverse, g_turn)
        for k in range(3):
            g_cam.append(found[4 * k + 3 : 4 * k + 4, :])
        g_cam.append(-sum(turn[k][0] * across_sum[k] + turn[k][1] * down_sum[k] for k in range(3)))
        for k in range(8):
            row = slice(k, k + 1)
            cam[row, :], cmean[row, :], csq[row, :] = adam(cam[row, :], g_cam[k], cmean[row, :], csq[row, :], first)
        for copy in lane_copies + edge_copies + back_copies:
            copy.wait_send()
        for copy in gathers:
            copy.wait()
        return carry

    loads[2].wait()
    loads[3].wait()
    lax.fori_loop(0, ITERS, iteration, 0)

    wait_small(small_send, 0, regions - 1)
    for phase in range(2 * ITERS):
        wait_messages(send_sem, phase)
    logd_out[...] = logd[ITERS]
    cam_out[...] = cam[:, 0:own]
    pose_out[...] = pose[:, 0:pairs]
    pmean_out[...] = pmean[:, 0:pairs]
    psq_out[...] = psq[:, 0:pairs]
    dmean_out[...] = dmean[...]
    dsq_out[...] = dsq[...]
    for src, dst in ((cmean, cmean_out), (csq, csq_out)):
        value = src[:, 0:share]
        for k in range(1, lanes):
            value = jnp.where(lane == k, src[:, k * share : (k + 1) * share], value)
        dst[...] = value


def shards(
    log_depth, cameras, pair_pose, depth_mean, depth_square, camera_mean, camera_square, pose_mean, pose_square,
    pointmaps, confidence, pair_images, pair_flag,
):
    regions = lax.axis_size("region")
    lanes = lax.axis_size("pair")
    own = log_depth.shape[0]
    pairs = pair_pose.shape[0]
    share = own // lanes
    slots = CAP * regions
    pair_rows = rounded(pairs, 8)
    pair_lanes = rounded(pairs, 128)
    keys = rounded(own + 16 + slots, 128)
    last = rounded(own + 16 + slots, 16)
    in_vmem = pl.BlockSpec(memory_space=pltpu.VMEM)
    anywhere = pl.BlockSpec(memory_space=pl.ANY)

    def vmem(*shape, dtype=F32):
        return pltpu.VMEM(shape, dtype)

    def out(*shape):
        return jax.ShapeDtypeStruct(shape, F32)

    results = pl.pallas_call(
        functools.partial(kernel, regions, lanes, own, pairs),
        out_shape=(
            out(own, ANCH), out(8, own), out(8, pairs), out(share, ANCH), out(share, ANCH),
            out(8, share), out(8, share), out(8, pairs), out(8, pairs),
        ),
        in_specs=[
            anywhere, in_vmem, in_vmem, anywhere, anywhere, in_vmem, in_vmem, in_vmem, in_vmem,
            anywhere, anywhere, in_vmem, in_vmem,
        ],
        out_specs=(in_vmem,) * 9,
        scratch_shapes=[
            vmem(ITERS + 1, own, ANCH), vmem(share, ANCH), vmem(share, ANCH),
            vmem(8, 128), vmem(8, 128), vmem(8, 128),
            vmem(8, pair_lanes), vmem(8, pair_lanes), vmem(8, pair_lanes),
            vmem(6, pairs, ANCH, dtype=BF16), vmem(2, pairs, ANCH, dtype=BF16),
            vmem(6, pair_rows, ANCH), vmem(2, pair_rows, ANCH),
            vmem(8, pair_lanes, dtype=jnp.int32),
            vmem(2, pair_rows, keys, dtype=BF16), vmem(keys, 2 * pair_lanes, dtype=BF16),
            vmem(slots, own, dtype=BF16), vmem(own, slots, dtype=BF16),
            vmem(3, keys, ANCH, dtype=BF16), vmem(keys, 128),
            vmem(2, pair_rows, ANCH), vmem(2, pair_rows, 128),
            vmem(2 * pair_lanes, ANCH), vmem(2, 2 * pair_lanes, 128), vmem(pair_lanes, 128),
            vmem(128, pair_lanes), vmem(128, 128), vmem(last, ANCH),
            vmem(regions, 8, 128), vmem(regions, 8, 128),
            vmem(ITERS, MSG * regions, 128), vmem(ITERS, MSG * regions, 128),
            vmem(ITERS, MSG * regions, 128), vmem(ITERS, MSG * regions, 128),
            vmem(ITERS, 2, EDGE, ANCH), vmem(ITERS, 2, EDGE, 128),
            vmem(ITERS, 2, EDGE, ANCH), vmem(ITERS, 2, EDGE, 128),
            vmem(ITERS, lanes - 1, share, ANCH), vmem(ITERS, lanes, 16, 128),
            pltpu.SemaphoreType.DMA((5,)),
            pltpu.SemaphoreType.DMA((2 * ITERS,)), pltpu.SemaphoreType.DMA((2 * ITERS,)),
            pltpu.SemaphoreType.DMA((1 + 16 * ITERS,)), pltpu.SemaphoreType.DMA((1 + 16 * ITERS,)),
        ],
        compiler_params=pltpu.CompilerParams(
            collective_id=0, has_side_effects=True, vmem_limit_bytes=48 * 1024 * 1024
        ),
        name="align",
    )(
        log_depth, cameras.T, pair_pose.T, depth_mean, depth_square, camera_mean.T, camera_square.T,
        pose_mean.T, pose_square.T, pointmaps.transpose(1, 0, 2), confidence.transpose(1, 0, 2),
        pair_images.T, pair_flag.reshape(1, pairs),
    )
    depth, camera, pose, dmean, dsq, cmean, csq, pmean, psq = results
    return depth, camera.T, pose.T, dmean, dsq, cmean.T, csq.T, pmean.T, psq.T


def solution(mesh):
    placed = (
        P("region", None),
        P("region", None),
        P(("region", "pair"), None),
        P("region", None),
        P("region", None),
        P("region", None),
        P("region", None),
        P(("region", "pair"), None),
        P(("region", "pair"), None),
        P(("region", "pair"), None, None),
        P(("region", "pair"), None, None),
        P(("region", "pair"), None),
        P(("region", "pair")),
    )
    return jax.shard_map(
        shards,
        mesh=mesh,
        in_specs=placed,
        out_specs=(
            P("region", None),
            P("region", None),
            P(("region", "pair"), None),
            P(("region", "pair"), None),
            P(("region", "pair"), None),
            P(("region", "pair"), None),
            P(("region", "pair"), None),
            P(("region", "pair"), None),
            P(("region", "pair"), None),
        ),
        check_vma=False,
    )
```

```python
import functools

import jax
import jax.numpy as jnp
from jax import lax
from jax.experimental import pallas as pl
from jax.experimental.pallas import tpu as pltpu
from jax.sharding import PartitionSpec as P

ANCH_W = 32
ANCH_H = 24
ANCH = 768
CAP = 2
NEIGHBOURS = 4
ITERS = 2
START = 300

LEARN_RATE = 0.01
BETA_ONE = 0.9
BETA_TWO = 0.999
EPSILON = 1e-08

TILES = ANCH // 128
EDGE = 8
MAPS = 4
MSG = TILES * CAP * MAPS
CHUNKS = 3
COEFS = 16
F32 = jnp.float32
BF16 = jnp.bfloat16


def rounded(value, multiple):
    return -(-value // multiple) * multiple


def split_two(x):
    high = x.astype(BF16)
    return high, (x - high.astype(F32)).astype(BF16)


def split_three(x):
    high = x.astype(BF16)
    rest = x - high.astype(F32)
    middle = rest.astype(BF16)
    return high, middle, (rest - middle.astype(F32)).astype(BF16)


def dot(a, b):
    return jnp.dot(a, b, preferred_element_type=F32)


def dot_exact(one_hot, x):
    high, middle, low = split_three(x)
    return dot(one_hot, high) + (dot(one_hot, middle) + dot(one_hot, low))


def pack_three(x):
    high, middle, low = split_three(x)
    rest = pltpu.roll(middle.astype(F32), COEFS, 1) + pltpu.roll(low.astype(F32), 2 * COEFS, 1)
    return (high.astype(F32) + rest).astype(BF16)


def rotation_rows(w, x, y, z):
    inverse = 1.0 / (w * w + x * x + y * y + z * z)
    matrix = [
        [w * w + x * x - y * y - z * z, 2.0 * (x * y - w * z), 2.0 * (x * z + w * y)],
        [2.0 * (x * y + w * z), w * w - x * x + y * y - z * z, 2.0 * (y * z - w * x)],
        [2.0 * (x * z - w * y), 2.0 * (y * z + w * x), w * w - x * x - y * y + z * z],
    ]
    return [[entry * inverse for entry in line] for line in matrix], inverse


def rotation_pull(q, matrix, inverse, g):
    w, x, y, z = q
    along = sum(g[k][j] * matrix[k][j] for k in range(3) for j in range(3))
    diag = g[0][0] + g[1][1] + g[2][2]
    g_w = w * diag + z * (g[1][0] - g[0][1]) + y * (g[0][2] - g[2][0]) + x * (g[2][1] - g[1][2])
    g_x = (
        x * (g[0][0] - g[1][1] - g[2][2])
        + y * (g[0][1] + g[1][0])
        + z * (g[0][2] + g[2][0])
        + w * (g[2][1] - g[1][2])
    )
    g_y = (
        y * (g[1][1] - g[0][0] - g[2][2])
        + x * (g[0][1] + g[1][0])
        + z * (g[1][2] + g[2][1])
        + w * (g[0][2] - g[2][0])
    )
    g_z = (
        z * (g[2][2] - g[0][0] - g[1][1])
        + x * (g[0][2] + g[2][0])
        + y * (g[1][2] + g[2][1])
        + w * (g[1][0] - g[0][1])
    )
    twice = 2.0 * inverse
    return [twice * (g_w - w * along), twice * (g_x - x * along), twice * (g_y - y * along), twice * (g_z - z * along)]


def adam(param, gradient, mean, square, first):
    fixes = [(1.0 - BETA_ONE ** (START + 1 + i), 1.0 - BETA_TWO ** (START + 1 + i)) for i in range(ITERS)]
    fix_one = jnp.where(first, F32(fixes[0][0]), F32(fixes[1][0]))
    fix_two = jnp.where(first, F32(fixes[0][1]), F32(fixes[1][1]))
    mean = BETA_ONE * mean + (1.0 - BETA_ONE) * gradient
    square = BETA_TWO * square + (1.0 - BETA_TWO) * gradient * gradient
    param = param - LEARN_RATE * (mean / fix_one) / (jnp.sqrt(square / fix_two) + EPSILON)
    return param, mean, square


def kernel(
    regions, lanes, own, pairs,
    logd_hbm, cam_hbm, pose_hbm, dmean_hbm, dsq_hbm, cmean_hbm, csq_hbm, pmean_hbm, psq_hbm, points_hbm, conf_hbm,
    images_hbm, flag_hbm,
    logd_out, cam_out, pose_out, dmean_out, dsq_out, cmean_out, csq_out, pmean_out, psq_out,
    cam_in, cmean_in, csq_in, pose_in, pmean_in, psq_in, images_in, flag_in,
    logd, dmean, dsq, cam, cmean, csq, pose, pmean, psq, points, conf, xs, cw,
    index_rows, pick_hot, back_hot, gather_hot, scatter_hot, camera_ones, pose_ones,
    table, small_table, rows_d, rows_c, rows_p, rows_g, rows_s, wide, narrow, grad_d, grad_s,
    small_out, small_in, bulk_out, bulk_in, first_out, first_in, second_out, second_in,
    edge_d, edge_c, back_d, back_c, part_d, part_c, moments,
    load_sem, send_sem, recv_sem, small_send, small_recv,
):
    share = own // lanes
    slots = CAP * regions
    nearby = pairs - CAP * (regions - 1)
    pair_lanes = pose.shape[1] - rounded(slots, 128)
    total_rows = pose.shape[1]
    near_at = pair_lanes - nearby
    keys = own + 16
    region = lax.axis_index("region")
    lane = lax.axis_index("pair")
    my_rows = pl.multiple_of(lane * share, share)

    def ahead(j):
        return lax.rem(region + j, regions)

    def behind(j):
        return lax.rem(region - j + regions, regions)

    def lane_at(k):
        return lax.rem(lane + k, lanes)

    loads = [
        pltpu.make_async_copy(src, dst, load_sem.at[n])
        for n, (src, dst) in enumerate(
            (
                (images_hbm, images_in), (flag_hbm, flag_in), (points_hbm, points), (conf_hbm, conf), (logd_hbm, logd.at[0]),
                (cam_hbm, cam_in), (cmean_hbm, cmean_in), (csq_hbm, csq_in),
                (pose_hbm, pose_in), (pmean_hbm, pmean_in), (psq_hbm, psq_in),
                (dmean_hbm.at[pl.ds(my_rows, share)], dmean), (dsq_hbm.at[pl.ds(my_rows, share)], dsq),
            )
        )
    ]
    for load in loads:
        load.start()

    barrier = pltpu.get_barrier_semaphore()

    def greet(j, carry):
        pl.semaphore_signal(barrier, inc=1, device_id={"region": ahead(j)})
        return carry

    lax.fori_loop(1, regions, greet, 0)
    for k in range(1, lanes):
        pl.semaphore_signal(barrier, inc=1, device_id={"pair": lane_at(k)})

    for load in loads:
        load.wait()

    def as_column(row):
        return jnp.transpose(jnp.broadcast_to(row, (128, row.shape[1])))[:, 0:1]

    lane_ids = lax.broadcasted_iota(jnp.int32, (1, pair_lanes), 1)
    index_rows[...] = jnp.zeros_like(index_rows)
    index_rows[0:2, 0:pairs] = images_in[...]
    index_rows[2:3, 0:pairs] = flag_in[...]
    real = lane_ids < pairs
    seconds = index_rows[1:2, :]
    flags = index_rows[2:3, :]
    remote = jnp.logical_and(flags == 1, real)
    firsts = jnp.where(real, index_rows[0:1, :] - region * own, 0).astype(F32)
    target = lax.div(seconds, jnp.full_like(seconds, own))
    local = seconds - target * own
    offset = target - region
    offset = jnp.where(offset < 0, offset + regions, offset)
    offset = jnp.where(remote, offset, 0).astype(F32)
    near = jnp.where(target == region, local, own + local).astype(F32)
    local = local.astype(F32)
    earlier_ids = lax.broadcasted_iota(jnp.int32, (pair_lanes, pair_lanes), 0)
    later_ids = lax.broadcasted_iota(jnp.int32, (pair_lanes, pair_lanes), 1)
    same = jnp.logical_and(as_column(offset) == offset, earlier_ids < later_ids)
    rank = jnp.sum(jnp.where(same, 1.0, 0.0), axis=0, keepdims=True)
    place = jnp.where(remote, rank * regions + offset - 1.0, slots + rank)
    place = jnp.where(real, place, -1.0)
    place_ids = lax.broadcasted_iota(jnp.int32, pick_hot.shape, 0).astype(F32)
    picked = place_ids == place
    pick_hot[...] = jnp.where(picked, 1.0, 0.0).astype(BF16)
    near = jnp.sum(jnp.where(picked, near, 0.0), axis=1, keepdims=True)[slots : slots + nearby]

    ones = jnp.ones((8, total_rows), F32)
    for padded, values in ((pose, pose_in), (pmean, pmean_in), (psq, psq_in)):
        padded[...] = ones
        padded[:, 0:pairs] = values[...]
    wide[...] = jnp.zeros_like(wide)
    wide[0:8, :] = pose[...]
    wide[8:16, :] = pmean[...]
    wide[16:24, :] = psq[...]
    wide[24:25, 0:pair_lanes] = local
    details = dot_exact(pick_hot[...], jnp.transpose(wide[:, 0:pair_lanes]))[0:slots]
    wide[...] = jnp.zeros_like(wide)

    def halves(values):
        return values[0:regions] + pltpu.roll(values[regions:slots], 64, 1)

    def from_halves(values):
        low = lax.broadcasted_iota(jnp.int32, values.shape, 1) < 64
        return jnp.concatenate([jnp.where(low, values, 0.0), jnp.where(low, pltpu.roll(values, 64, 1), 0.0)], 0)

    small_out[...] = halves(details)
    small_in[regions - 1 : regions, :] = jnp.ones((1, 128), F32)
    weights = 2.0 * (1.0 + flags.astype(F32))
    weights = jnp.where(real, weights, 0.0)
    weight_column = as_column(weights)
    slot_weights = jnp.sum(jnp.where(picked, weights, 0.0), axis=1, keepdims=True)
    xs[...] = jnp.zeros_like(xs)
    cw[...] = jnp.zeros_like(cw)
    for m in range(MAPS):
        source = points[3 + m] if m < 3 else conf[1]
        chosen = dot(pick_hot[:, 0:pairs], source)
        if m == 3:
            chosen = chosen * slot_weights
        for c in range(CAP):
            for g in range(regions // 8):
                rows = slice(c * regions + 8 * g, c * regions + 8 * g + 8)
                for t in range(TILES):
                    at = MSG * 8 * g + CAP * MAPS * t + MAPS * c + m
                    bulk_out[pl.ds(at, 8, stride=MSG), :] = chosen[rows, 128 * t : 128 * t + 128]
        if m < 3:
            xs[m, near_at:pair_lanes, :] = chosen[slots : slots + nearby]
        else:
            cw[near_at:pair_lanes, :] = chosen[slots : slots + nearby]

    def send_row(src, dst, which, j, to):
        at = pl.ds(j - 1, 1)
        pltpu.make_async_remote_copy(
            src_ref=src.at[at],
            dst_ref=dst.at[at],
            send_sem=send_sem.at[which],
            recv_sem=recv_sem.at[which],
            device_id={"region": to},
        ).start()

    def wait_rows(sem, which, count):
        whole = bulk_in.at[pl.ds(0, count)]
        pltpu.make_async_copy(whole, whole, sem.at[which]).wait()

    pl.semaphore_wait(barrier, regions - 1 + lanes - 1)

    def send_small(j, carry):
        send_row(small_out, small_in, 0, j, ahead(j))
        return carry

    lax.fori_loop(1, regions, send_small, 0)
    chunk = MSG // CHUNKS
    for h in range(CHUNKS):

        def send_chunk(j, carry, h=h):
            at = pl.ds(pl.multiple_of((j - 1) * MSG + h * chunk, 8), chunk)
            pltpu.make_async_remote_copy(
                src_ref=bulk_out.at[at],
                dst_ref=bulk_in.at[at],
                send_sem=send_sem.at[1 + h],
                recv_sem=recv_sem.at[1 + h],
                device_id={"region": ahead(j)},
            ).start()
            return carry

        def send_both(j, carry, send_chunk=send_chunk):
            return send_chunk(regions - j, send_chunk(j, carry))

        lax.fori_loop(1, regions // 2, send_both, 0)
        send_chunk(regions // 2, 0)

    for m in range(3):
        xs[m, 0:pairs, :] = points[m].astype(F32)
    cw[0:pairs, :] = conf[0].astype(F32) * weight_column[0:pairs]
    def one_hots(column, count):
        key_ids = lax.broadcasted_iota(jnp.int32, (count, gather_hot.shape[1]), 1)
        for n in (2, 1):
            key_ids = jnp.where(key_ids >= n * keys, jnp.where(key_ids < 3 * keys, key_ids - n * keys, -1), key_ids)
        return jnp.where(column == key_ids.astype(F32), 1.0, 0.0)

    hot = one_hots(jnp.concatenate([as_column(firsts)[0:near_at], near], 0), pair_lanes)
    gather_hot[0:pair_lanes, :] = hot.astype(BF16)
    scatter_hot[:, 0:pair_lanes] = jnp.transpose(hot[:, 0:128]).astype(BF16)
    place_ids = lax.broadcasted_iota(jnp.int32, back_hot.shape, 1).astype(F32)
    back_hot[...] = jnp.where(as_column(place) == place_ids, 1.0, 0.0).astype(BF16)

    column_ids = lax.broadcasted_iota(jnp.int32, (8, 128), 1)
    down_step = 8.0 * (128 // ANCH_W)
    row_ids = lax.broadcasted_iota(jnp.int32, (128, 128), 0)
    anchor = lax.broadcasted_iota(jnp.int32, (128, 128), 1)
    anchor_row = lax.div(anchor, jnp.full_like(anchor, ANCH_W))
    across = (8 * (anchor - anchor_row * ANCH_W) + 4 - 4 * ANCH_W).astype(F32)
    downward = (8 * anchor_row + 4 - 4 * ANCH_H).astype(F32)
    kind = lax.rem(row_ids, jnp.full_like(row_ids, COEFS))
    kind = jnp.where(row_ids < 3 * COEFS, kind, -1)
    for k in range(3):
        ray = jnp.where(kind == 4 * k, across, jnp.where(kind == 4 * k + 1, downward, jnp.where(kind == 4 * k + 2, 1.0, 0.0)))
        step = jnp.where(kind == 4 * k + 1, down_step, 0.0)
        move = jnp.where(kind == 4 * k + 3, 1.0, 0.0)
        for b, value in ((k, ray), (3 + k, step), (6 + k, move)):
            camera_ones[:, 128 * b : 128 * b + 128] = value.astype(BF16)
        for j in range(4):
            b = 4 * k + j
            pose_ones[:, 128 * b : 128 * b + 128] = jnp.where(kind == b, 1.0, 0.0).astype(BF16)
    across = across[0:8, :]
    downward = downward[0:8, :]

    for padded, values in ((cam, cam_in), (cmean, cmean_in), (csq, csq_in)):
        padded[...] = jnp.ones((8, 128), F32)
        padded[:, 0:own] = values[...]
    narrow[...] = jnp.zeros_like(narrow)
    rows_g[...] = jnp.zeros_like(rows_g)
    rows_s[...] = jnp.zeros_like(rows_s)
    table[...] = jnp.zeros_like(table)
    small_table[...] = jnp.zeros_like(small_table)

    def small_copy(it, phase, src, dst, device_id):
        return pltpu.make_async_remote_copy(
            src_ref=src,
            dst_ref=dst,
            send_sem=small_send.at[16 * it + phase],
            recv_sem=small_recv.at[16 * it + phase],
            device_id=device_id,
        )

    def fill_table(at, depth, coefs):
        for n, piece in enumerate(split_three(depth)):
            table[n * keys + at : n * keys + at + depth.shape[0], :] = piece
        for n, piece in enumerate(split_three(coefs)):
            small_table[n * keys + at : n * keys + at + depth.shape[0], :] = piece

    def gather(at, count):
        hot = gather_hot[at : at + count, :]
        for n in range(0, ANCH, 256):
            rows_d[at : at + count, n : n + 256] = dot(hot, table[:, n : n + 256])
        rows_c[at : at + count, :] = dot(pack_three(dot(hot, small_table[...])), camera_ones[...])

    def pose_rows(at, values):
        rows_p[at : at + values.shape[0], :] = dot(pack_three(values), pose_ones[...])

    def group(g, inner):
        at = pl.ds(pl.multiple_of(g * 8, 8), 8)

        def block(ref, b):
            return ref[at, 128 * b : 128 * b + 128]

        shift = [[block(rows_p, 4 * k + j) for j in range(4)] for k in range(3)]
        ray = [block(rows_c, k) for k in range(3)]
        zero = jnp.zeros((8, 128), F32)
        turned = [[zero for j in range(3)] for k in range(3)]
        total = [zero for k in range(3)]
        by_depth = [zero for k in range(3)]
        by_down = [zero for k in range(3)]
        for t in range(TILES):
            part = slice(128 * t, 128 * t + 128)
            d = rows_d[at, part]
            c = cw[at, part]
            x = [xs[j, at, part] for j in range(3)]
            along = None
            for k in range(3):
                placed = shift[k][0] * x[0] + shift[k][1] * x[1] + (shift[k][2] * x[2] + shift[k][3])
                pull = c * ((d * ray[k] + block(rows_c, 6 + k)) - placed)
                for j in range(3):
                    turned[k][j] = turned[k][j] + pull * x[j]
                total[k] = total[k] + pull
                deep = pull * d
                by_depth[k] = by_depth[k] + deep
                if t > 0:
                    by_down[k] = by_down[k] + F32(t) * deep
                along = deep * ray[k] if along is None else along + deep * ray[k]
                if t < TILES - 1:
                    ray[k] = ray[k] + block(rows_c, 3 + k)
            rows_g[at, part] = along
        out = zero
        for k in range(3):
            values = [by_depth[k] * across, by_depth[k] * downward + by_down[k] * down_step, by_depth[k], total[k]]
            for j in range(4):
                out = jnp.where(column_ids == 4 * k + j, jnp.sum(values[j], axis=1, keepdims=True), out)
            for j in range(3):
                column = COEFS + 4 * k + j
                out = jnp.where(column_ids == column, jnp.sum(turned[k][j], axis=1, keepdims=True), out)
        rows_s[at, :] = out
        return inner

    def iteration(it, carry):
        first = it == 0
        q = [cam[k : k + 1, :] for k in range(4)]
        turn, turn_inverse = rotation_rows(*q)
        near_focal = jnp.exp(-cam[7:8, :])
        for k in range(3):
            narrow[4 * k : 4 * k + 1, :] = turn[k][0] * near_focal
            narrow[4 * k + 1 : 4 * k + 2, :] = turn[k][1] * near_focal
            narrow[4 * k + 2 : 4 * k + 3, :] = turn[k][2]
            narrow[4 * k + 3 : 4 * k + 4, :] = cam[4 + k : 5 + k, :]
        coefs = jnp.transpose(narrow[...])[0:own, :]
        depth = jnp.exp(logd[it])
        edge_d[it, 0] = depth[0:EDGE, :]
        edge_c[it, 0] = coefs[0:EDGE, :]
        edge_copies = [
            small_copy(it, 0, edge_d.at[it, 0], edge_d.at[it, 1], {"region": behind(1)}),
            small_copy(it, 1, edge_c.at[it, 0], edge_c.at[it, 1], {"region": behind(1)}),
        ]
        for copy in edge_copies:
            copy.start()
        fill_table(0, depth, coefs)
        gather(0, near_at)

        def pair_coefs():
            p = [pose[k : k + 1, :] for k in range(4)]
            bend, bend_inverse = rotation_rows(*p)
            scale = jnp.exp(pose[7:8, :])
            for k in range(3):
                for j in range(3):
                    wide[4 * k + j : 4 * k + j + 1, :] = scale * bend[k][j]
                wide[4 * k + 3 : 4 * k + 4, :] = scale * pose[4 + k : 5 + k, :]
            return jnp.transpose(wide[...])

        @pl.when(first)
        def _():
            values = pair_coefs()
            near_values = dot_exact(pick_hot[slots : slots + nearby, :], values[0:pair_lanes])
            pose_rows(0, jnp.concatenate([values[0:near_at], near_values], 0))

        lax.fori_loop(0, near_at // 8, group, 0)

        @pl.when(first)
        def _():
            found = dot_exact(pick_hot[0:slots, :], rows_s[0:pair_lanes, :])
            first_out[...] = halves(found)

            def send(j, inner):
                send_row(first_out, first_in, 1 + CHUNKS, j, ahead(j))
                return inner

            lax.fori_loop(1, regions, send, 0)

        for copy in edge_copies:
            copy.wait_recv()
        fill_table(
            own,
            jnp.concatenate([edge_d[it, 1], jnp.zeros((8, ANCH), F32)], 0),
            jnp.concatenate([edge_c[it, 1], jnp.zeros((8, 128), F32)], 0),
        )
        gather(near_at, nearby)
        lax.fori_loop(near_at // 8, pair_lanes // 8, group, 0)
        hot = scatter_hot[0:keys, 0:pair_lanes]
        for n in range(0, ANCH, 256):
            high, low = split_two(rows_g[0:pair_lanes, n : n + 256])
            grad_d[:, n : n + 256] = dot(hot, high) + dot(hot, low)
        grad_s[...] = dot_exact(hot, rows_s[0:pair_lanes, :])
        back_d[it, 0] = grad_d[own : own + EDGE, :]
        back_c[it, 0] = grad_s[own : own + EDGE, :]
        back_copies = [
            small_copy(it, 2, back_d.at[it, 0], back_d.at[it, 1], {"region": ahead(1)}),
            small_copy(it, 3, back_c.at[it, 0], back_c.at[it, 1], {"region": ahead(1)}),
        ]
        for copy in back_copies:
            copy.start()

        @pl.when(first)
        def _():
            wait_rows(recv_sem, 0, regions - 1)
            named = from_halves(small_in[...])
            hot = one_hots(named[:, 24:25], slots)
            gather_hot[pair_lanes : pair_lanes + slots, :] = hot.astype(BF16)
            if slots < 128:
                hot = jnp.concatenate([hot, jnp.zeros((128 - slots, hot.shape[1]), F32)], 0)
                named = jnp.concatenate([named, jnp.ones((128 - slots, 128), F32)], 0)
            scatter_hot[:, pair_lanes:total_rows] = jnp.transpose(hot[:, 0:128]).astype(BF16)
            named = jnp.transpose(named)
            pose[:, pair_lanes:total_rows] = named[0:8, :]
            pmean[:, pair_lanes:total_rows] = named[8:16, :]
            psq[:, pair_lanes:total_rows] = named[16:24, :]
            values = pair_coefs()
            pose_rows(pair_lanes, values[pair_lanes : pair_lanes + slots])
            for h in range(CHUNKS):
                wait_rows(recv_sem, 1 + h, chunk * (regions - 1))
            bulk_in[MSG * (regions - 1) : MSG * regions, :] = jnp.zeros((MSG, 128), F32)
            for c in range(CAP):
                for g in range(regions // 8):
                    at = pair_lanes + c * regions + 8 * g
                    for t in range(TILES):
                        for m in range(MAPS):
                            source = MSG * 8 * g + CAP * MAPS * t + MAPS * c + m
                            value = bulk_in[pl.ds(source, 8, stride=MSG), :]
                            if m < 3:
                                xs[m, at : at + 8, 128 * t : 128 * t + 128] = value
                            else:
                                cw[at : at + 8, 128 * t : 128 * t + 128] = value

        gather(pair_lanes, slots)
        lax.fori_loop(pair_lanes // 8, (pair_lanes + slots) // 8, group, 0)
        second_out[it] = halves(rows_s[pair_lanes : pair_lanes + slots, :])

        def send_back(j, inner):
            send_row(second_out.at[it], second_in.at[it], 2 + CHUNKS + it, j, behind(j))
            return inner

        lax.fori_loop(1, regions, send_back, 0)
        hot = scatter_hot[0:own, pair_lanes:total_rows]
        for n in range(0, ANCH, 256):
            high, low = split_two(rows_g[pair_lanes:total_rows, n : n + 256])
            grad_d[0:own, n : n + 256] = grad_d[0:own, n : n + 256] + (dot(hot, high) + dot(hot, low))
        sums = grad_s[0:own, :] + dot_exact(hot, rows_s[pair_lanes:total_rows, :])
        for copy in back_copies:
            copy.wait_recv()
        grad_d[0:EDGE, :] = grad_d[0:EDGE, :] + back_d[it, 1]
        sums = jnp.concatenate([sums[0:EDGE, :] + back_c[it, 1], sums[EDGE:own, :]], 0)
        if own < 128:
            sums = jnp.concatenate([sums, jnp.zeros((128 - own, 128), F32)], 0)
        part_c[it, lane] = jnp.transpose(sums)[0:16, :]

        lane_copies = []
        for k in range(1, lanes):
            to = lane_at(k)
            rows = pl.ds(pl.multiple_of(to * share, share), share)
            lane_copies.append(small_copy(it, 4 + k, grad_d.at[rows], part_d.at[it, k - 1], {"pair": to}))
            lane_copies.append(small_copy(it, 7 + k, part_c.at[it, lane], part_c.at[it, lane], {"pair": to}))
        for copy in lane_copies:
            copy.start()
        for copy in lane_copies:
            copy.wait_recv()
        gradient = grad_d[pl.ds(my_rows, share), :]
        for k in range(1, lanes):
            gradient = gradient + part_d[it, k - 1]
        updated, dmean[...], dsq[...] = adam(logd[it, pl.ds(my_rows, share), :], gradient, dmean[...], dsq[...], first)
        logd[it + 1, pl.ds(my_rows, share), :] = updated
        mine = logd.at[it + 1, pl.ds(my_rows, share)]
        gathers = [small_copy(it, 10 + k, mine, mine, {"pair": lane_at(k)}) for k in range(1, lanes)]
        for copy in gathers:
            copy.start()

        found = part_c[it, 0]
        for k in range(1, lanes):
            found = found + part_c[it, k]
        across_sum = [found[4 * k : 4 * k + 1, :] * near_focal for k in range(3)]
        down_sum = [found[4 * k + 1 : 4 * k + 2, :] * near_focal for k in range(3)]
        g_turn = [[across_sum[k], down_sum[k], found[4 * k + 2 : 4 * k + 3, :]] for k in range(3)]
        g_cam = rotation_pull(q, turn, turn_inverse, g_turn)
        for k in range(3):
            g_cam.append(found[4 * k + 3 : 4 * k + 4, :])
        g_cam.append(-sum(turn[k][0] * across_sum[k] + turn[k][1] * down_sum[k] for k in range(3)))
        for k in range(8):
            row = slice(k, k + 1)
            cam[row, :], cmean[row, :], csq[row, :] = adam(cam[row, :], g_cam[k], cmean[row, :], csq[row, :], first)

        @pl.when(first)
        def _():
            wait_rows(recv_sem, 1 + CHUNKS, regions - 1)
            first_in[regions - 1 : regions, :] = jnp.zeros((1, 128), F32)

        wait_rows(recv_sem, 2 + CHUNKS + it, regions - 1)
        second_in[it, regions - 1 : regions, :] = jnp.zeros((1, 128), F32)
        seconds = jnp.concatenate([from_halves(second_in[it]), rows_s[near_at:pair_lanes, :]], 0)
        of_pairs = dot_exact(back_hot[...], seconds)
        of_pairs = jnp.concatenate([of_pairs[0:near_at] + rows_s[0:near_at, :], of_pairs[near_at:pair_lanes]], 0)
        of_slots = from_halves(first_in[...]) + rows_s[pair_lanes : pair_lanes + slots, :]
        if slots < total_rows - pair_lanes:
            of_slots = jnp.concatenate([of_slots, jnp.zeros((total_rows - pair_lanes - slots, 128), F32)], 0)
        found = jnp.transpose(jnp.concatenate([of_pairs, of_slots], 0))
        m = [[found[COEFS + 4 * k + j : COEFS + 4 * k + j + 1, :] for j in range(3)] for k in range(3)]
        v = [found[4 * k + 3 : 4 * k + 4, :] for k in range(3)]
        p = [pose[k : k + 1, :] for k in range(4)]
        bend, bend_inverse = rotation_rows(*p)
        scale = jnp.exp(pose[7:8, :])
        g_turn = [[-(scale * m[k][j]) for j in range(3)] for k in range(3)]
        g_pose = rotation_pull(p, bend, bend_inverse, g_turn)
        g_scale = sum(bend[k][j] * g_turn[k][j] for k in range(3) for j in range(3))
        for k in range(3):
            g_move = -(scale * v[k])
            g_scale = g_scale + pose[4 + k : 5 + k, :] * g_move
            g_pose.append(g_move)
        g_pose.append(g_scale)
        for k in range(8):
            row = slice(k, k + 1)
            pose[row, :], pmean[row, :], psq[row, :] = adam(pose[row, :], g_pose[k], pmean[row, :], psq[row, :], first)

        @pl.when(it < ITERS - 1)
        def _():
            values = pair_coefs()
            near_values = dot_exact(pick_hot[slots : slots + nearby, :], values[0:pair_lanes])
            pose_rows(0, jnp.concatenate([values[0:near_at], near_values, values[pair_lanes : pair_lanes + slots]], 0))

        for copy in lane_copies + edge_copies + back_copies:
            copy.wait_send()
        for copy in gathers:
            copy.wait()
        return carry

    lax.fori_loop(0, ITERS, iteration, 0)

    wait_rows(send_sem, 0, regions - 1)
    for h in range(CHUNKS):
        wait_rows(send_sem, 1 + h, chunk * (regions - 1))
    for n in range(1 + ITERS):
        wait_rows(send_sem, 1 + CHUNKS + n, regions - 1)
    cam_in[...] = cam[:, 0:own]
    pose_in[...] = pose[:, 0:pairs]
    pmean_in[...] = pmean[:, 0:pairs]
    psq_in[...] = psq[:, 0:pairs]
    for n, src in enumerate((cmean, csq)):
        value = src[:, 0:share]
        for k in range(1, lanes):
            value = jnp.where(lane == k, src[:, k * share : (k + 1) * share], value)
        moments[n] = value
    stores = [
        pltpu.make_async_copy(src, dst, load_sem.at[n])
        for n, (src, dst) in enumerate(
            (
                (logd.at[ITERS], logd_out), (cam_in, cam_out), (pose_in, pose_out), (dmean, dmean_out), (dsq, dsq_out),
                (moments.at[0], cmean_out), (moments.at[1], csq_out), (pmean_in, pmean_out), (psq_in, psq_out),
            )
        )
    ]
    for store in stores:
        store.start()
    for store in stores:
        store.wait()


def deliver(*refs):
    count = (len(refs) - 1) // 2
    copies = [pltpu.make_async_copy(refs[n], refs[count + n], refs[-1].at[n]) for n in range(count)]
    for copy in copies:
        copy.start()
    for copy in copies:
        copy.wait()


def shards(
    log_depth, cameras, pair_pose, depth_mean, depth_square, camera_mean, camera_square, pose_mean, pose_square,
    pointmaps, confidence, pair_images, pair_flag,
):
    regions = lax.axis_size("region")
    lanes = lax.axis_size("pair")
    own = log_depth.shape[0]
    pairs = pair_pose.shape[0]
    share = own // lanes
    slots = CAP * regions
    nearby = pairs - CAP * (regions - 1)
    pair_lanes = rounded(pairs, 128)
    total_rows = pair_lanes + rounded(slots, 128)
    keys = own + 16
    key_lanes = rounded(3 * keys, 128)
    in_hbm = pl.BlockSpec(memory_space=pltpu.HBM)

    def vmem(*shape, dtype=F32):
        return pltpu.VMEM(shape, dtype)

    def out(*shape):
        return jax.ShapeDtypeStruct(shape, F32)

    shapes = (
        out(own, ANCH), out(8, own), out(8, pairs), out(share, ANCH), out(share, ANCH),
        out(8, share), out(8, share), out(8, pairs), out(8, pairs),
    )
    results = pl.pallas_call(
        functools.partial(kernel, regions, lanes, own, pairs),
        out_shape=shapes,
        in_specs=[in_hbm] * 13,
        out_specs=(in_hbm,) * 9,
        scratch_shapes=[
            vmem(8, own), vmem(8, own), vmem(8, own), vmem(8, pairs), vmem(8, pairs), vmem(8, pairs),
            vmem(2, pairs, dtype=jnp.int32), vmem(1, pairs, dtype=jnp.int32),
            vmem(ITERS + 1, own, ANCH), vmem(share, ANCH), vmem(share, ANCH),
            vmem(8, 128), vmem(8, 128), vmem(8, 128),
            vmem(8, total_rows), vmem(8, total_rows), vmem(8, total_rows),
            vmem(6, pairs, ANCH, dtype=BF16), vmem(2, pairs, ANCH, dtype=BF16),
            vmem(3, total_rows, ANCH), vmem(total_rows, ANCH),
            vmem(8, pair_lanes, dtype=jnp.int32),
            vmem(slots + nearby, pair_lanes, dtype=BF16), vmem(pair_lanes, slots + nearby, dtype=BF16),
            vmem(total_rows, key_lanes, dtype=BF16), vmem(128, total_rows, dtype=BF16),
            vmem(128, 9 * 128, dtype=BF16), vmem(128, 12 * 128, dtype=BF16),
            vmem(key_lanes, ANCH, dtype=BF16), vmem(key_lanes, 128, dtype=BF16),
            vmem(total_rows, ANCH), vmem(total_rows, 9 * 128), vmem(total_rows, 12 * 128),
            vmem(total_rows, ANCH), vmem(total_rows, 128),
            vmem(128, total_rows), vmem(128, 128), vmem(keys, ANCH), vmem(keys, 128),
            vmem(regions, 128), vmem(regions, 128), vmem(MSG * regions, 128), vmem(MSG * regions, 128),
            vmem(regions, 128), vmem(regions, 128), vmem(ITERS, regions, 128), vmem(ITERS, regions, 128),
            vmem(ITERS, 2, EDGE, ANCH), vmem(ITERS, 2, EDGE, 128),
            vmem(ITERS, 2, EDGE, ANCH), vmem(ITERS, 2, EDGE, 128),
            vmem(ITERS, lanes - 1, share, ANCH), vmem(ITERS, lanes, 16, 128), vmem(2, 8, share),
            pltpu.SemaphoreType.DMA((13,)),
            pltpu.SemaphoreType.DMA((2 + CHUNKS + ITERS,)), pltpu.SemaphoreType.DMA((2 + CHUNKS + ITERS,)),
            pltpu.SemaphoreType.DMA((16 * ITERS,)), pltpu.SemaphoreType.DMA((16 * ITERS,)),
        ],
        compiler_params=pltpu.CompilerParams(
            collective_id=0, has_side_effects=True, vmem_limit_bytes=62 * 1024 * 1024
        ),
        name="align",
    )(
        log_depth, cameras.T, pair_pose.T, depth_mean, depth_square, camera_mean.T, camera_square.T,
        pose_mean.T, pose_square.T, pointmaps.transpose(1, 0, 2), confidence.transpose(1, 0, 2),
        pair_images.T, pair_flag.reshape(1, pairs),
    )
    depth, camera, pose, dmean, dsq, cmean, csq, pmean, psq = pl.pallas_call(
        deliver,
        out_shape=shapes,
        in_specs=[in_hbm] * 9,
        out_specs=(in_hbm,) * 9,
        scratch_shapes=[pltpu.SemaphoreType.DMA((9,))],
        compiler_params=pltpu.CompilerParams(vmem_limit_bytes=62 * 1024 * 1024),
        name="deliver",
    )(*results)
    return depth, camera.T, pose.T, dmean, dsq, cmean.T, csq.T, pmean.T, psq.T


def solution(mesh):
    placed = (
        P("region", None),
        P("region", None),
        P(("region", "pair"), None),
        P("region", None),
        P("region", None),
        P("region", None),
        P("region", None),
        P(("region", "pair"), None),
        P(("region", "pair"), None),
        P(("region", "pair"), None, None),
        P(("region", "pair"), None, None),
        P(("region", "pair"), None),
        P(("region", "pair")),
    )
    return jax.shard_map(
        shards,
        mesh=mesh,
        in_specs=placed,
        out_specs=(
            P("region", None),
            P("region", None),
            P(("region", "pair"), None),
            P(("region", "pair"), None),
            P(("region", "pair"), None),
            P(("region", "pair"), None),
            P(("region", "pair"), None),
            P(("region", "pair"), None),
            P(("region", "pair"), None),
        ),
        check_vma=False,
    )
```

```python
import functools

import jax
import jax.numpy as jnp
from jax import lax
from jax.experimental import pallas as pl
from jax.experimental.pallas import tpu as pltpu
from jax.sharding import PartitionSpec as P

ANCH_W = 32
ANCH_H = 24
ANCH = 768
CAP = 2
NEIGHBOURS = 4
ITERS = 2
START = 300

LEARN_RATE = 0.01
BETA_ONE = 0.9
BETA_TWO = 0.999
EPSILON = 1e-08

TILES = ANCH // 128
EDGE = 8
MAPS = 4
MSG = TILES * CAP * MAPS
CHUNKS = 3
COEFS = 16
F32 = jnp.float32
BF16 = jnp.bfloat16


def rounded(value, multiple):
    return -(-value // multiple) * multiple


def split_two(x):
    high = x.astype(BF16)
    return high, (x - high.astype(F32)).astype(BF16)


def split_three(x):
    high = x.astype(BF16)
    rest = x - high.astype(F32)
    middle = rest.astype(BF16)
    return high, middle, (rest - middle.astype(F32)).astype(BF16)


def dot(a, b):
    return jnp.dot(a, b, preferred_element_type=F32)


def dot_exact(one_hot, x):
    high, middle, low = split_three(x)
    return dot(one_hot, high) + (dot(one_hot, middle) + dot(one_hot, low))


def pack_three(x):
    high, middle, low = split_three(x)
    rest = pltpu.roll(middle.astype(F32), COEFS, 1) + pltpu.roll(low.astype(F32), 2 * COEFS, 1)
    return (high.astype(F32) + rest).astype(BF16)


def rotation_rows(w, x, y, z):
    inverse = 1.0 / (w * w + x * x + y * y + z * z)
    matrix = [
        [w * w + x * x - y * y - z * z, 2.0 * (x * y - w * z), 2.0 * (x * z + w * y)],
        [2.0 * (x * y + w * z), w * w - x * x + y * y - z * z, 2.0 * (y * z - w * x)],
        [2.0 * (x * z - w * y), 2.0 * (y * z + w * x), w * w - x * x - y * y + z * z],
    ]
    return [[entry * inverse for entry in line] for line in matrix], inverse


def rotation_pull(q, matrix, inverse, g):
    w, x, y, z = q
    along = sum(g[k][j] * matrix[k][j] for k in range(3) for j in range(3))
    diag = g[0][0] + g[1][1] + g[2][2]
    g_w = w * diag + z * (g[1][0] - g[0][1]) + y * (g[0][2] - g[2][0]) + x * (g[2][1] - g[1][2])
    g_x = (
        x * (g[0][0] - g[1][1] - g[2][2])
        + y * (g[0][1] + g[1][0])
        + z * (g[0][2] + g[2][0])
        + w * (g[2][1] - g[1][2])
    )
    g_y = (
        y * (g[1][1] - g[0][0] - g[2][2])
        + x * (g[0][1] + g[1][0])
        + z * (g[1][2] + g[2][1])
        + w * (g[0][2] - g[2][0])
    )
    g_z = (
        z * (g[2][2] - g[0][0] - g[1][1])
        + x * (g[0][2] + g[2][0])
        + y * (g[1][2] + g[2][1])
        + w * (g[1][0] - g[0][1])
    )
    twice = 2.0 * inverse
    return [twice * (g_w - w * along), twice * (g_x - x * along), twice * (g_y - y * along), twice * (g_z - z * along)]


def adam(param, gradient, mean, square, it):
    fix_one = 1.0 - BETA_ONE ** (START + 1 + it)
    fix_two = 1.0 - BETA_TWO ** (START + 1 + it)
    mean = BETA_ONE * mean + (1.0 - BETA_ONE) * gradient
    square = BETA_TWO * square + (1.0 - BETA_TWO) * gradient * gradient
    param = param - LEARN_RATE * (mean / fix_one) / (jnp.sqrt(square / fix_two) + EPSILON)
    return param, mean, square


def kernel(
    regions, lanes, own, pairs,
    logd_hbm, cam_hbm, pose_hbm, dmean_hbm, dsq_hbm, cmean_hbm, csq_hbm, pmean_hbm, psq_hbm, points_hbm, conf_hbm,
    images_hbm, flag_hbm,
    logd_out, cam_out, pose_out, dmean_out, dsq_out, cmean_out, csq_out, pmean_out, psq_out,
    cam_in, cmean_in, csq_in, pose_in, pmean_in, psq_in, images_in, flag_in,
    logd, dmean, dsq, cam, cmean, csq, pose, pmean, psq, points, conf, xs, cw,
    index_rows, pick_hot, back_hot, gather_hot, scatter_hot, camera_ones, pose_ones,
    table, small_table, rows_d, rows_c, rows_p, rows_g, rows_s, wide, narrow, grad_d, grad_s,
    small_out, small_in, bulk_out, bulk_in, first_out, first_in, second_out, second_in,
    edge_d, edge_c, back_d, back_c, part_d, part_e, part_c, moments,
    load_sem, send_sem, recv_sem, small_send, small_recv,
):
    share = own // lanes
    slots = CAP * regions
    nearby = pairs - CAP * (regions - 1)
    pair_lanes = pose.shape[1] - rounded(slots, 128)
    total_rows = pose.shape[1]
    near_at = pair_lanes - nearby
    keys = own + 16
    region = lax.axis_index("region")
    lane = lax.axis_index("pair")
    my_rows = pl.multiple_of(lane * share, share)

    def ahead(j):
        return lax.rem(region + j, regions)

    def behind(j):
        return lax.rem(region - j + regions, regions)

    def lane_at(k):
        return lax.rem(lane + k, lanes)

    loads = [
        pltpu.make_async_copy(src, dst, load_sem.at[n])
        for n, (src, dst) in enumerate(
            (
                (images_hbm, images_in), (flag_hbm, flag_in), (points_hbm, points), (conf_hbm, conf), (logd_hbm, logd.at[0]),
                (cam_hbm, cam_in), (cmean_hbm, cmean_in), (csq_hbm, csq_in),
                (pose_hbm, pose_in), (pmean_hbm, pmean_in), (psq_hbm, psq_in),
                (dmean_hbm.at[pl.ds(my_rows, share)], dmean), (dsq_hbm.at[pl.ds(my_rows, share)], dsq),
            )
        )
    ]
    for load in loads:
        load.start()

    barrier = pltpu.get_barrier_semaphore()

    def greet(j, carry):
        pl.semaphore_signal(barrier, inc=1, device_id={"region": ahead(j)})
        return carry

    lax.fori_loop(1, regions, greet, 0)
    for k in range(1, lanes):
        pl.semaphore_signal(barrier, inc=1, device_id={"pair": lane_at(k)})


    @pl.when(lane == 0)
    def _():
        for k in range(1, lanes):
            pl.semaphore_signal(barrier, inc=1, device_id={"region": behind(1), "pair": k})

    for load in loads:
        load.wait()

    def as_column(row):
        return jnp.transpose(jnp.broadcast_to(row, (128, row.shape[1])))[:, 0:1]

    lane_ids = lax.broadcasted_iota(jnp.int32, (1, pair_lanes), 1)
    index_rows[...] = jnp.zeros_like(index_rows)
    index_rows[0:2, 0:pairs] = images_in[...]
    index_rows[2:3, 0:pairs] = flag_in[...]
    real = lane_ids < pairs
    seconds = index_rows[1:2, :]
    flags = index_rows[2:3, :]
    remote = jnp.logical_and(flags == 1, real)
    firsts = jnp.where(real, index_rows[0:1, :] - region * own, 0).astype(F32)
    target = lax.div(seconds, jnp.full_like(seconds, own))
    local = seconds - target * own
    offset = target - region
    offset = jnp.where(offset < 0, offset + regions, offset)
    offset = jnp.where(remote, offset, 0).astype(F32)
    near = jnp.where(target == region, local, own + local).astype(F32)
    local = local.astype(F32)
    earlier_ids = lax.broadcasted_iota(jnp.int32, (pair_lanes, pair_lanes), 0)
    later_ids = lax.broadcasted_iota(jnp.int32, (pair_lanes, pair_lanes), 1)
    same = jnp.logical_and(as_column(offset) == offset, earlier_ids < later_ids)
    rank = jnp.sum(jnp.where(same, 1.0, 0.0), axis=0, keepdims=True)
    place = jnp.where(remote, rank * regions + offset - 1.0, slots + rank)
    place = jnp.where(real, place, -1.0)
    place_ids = lax.broadcasted_iota(jnp.int32, pick_hot.shape, 0).astype(F32)
    picked = place_ids == place
    pick_hot[...] = jnp.where(picked, 1.0, 0.0).astype(BF16)
    near = jnp.sum(jnp.where(picked, near, 0.0), axis=1, keepdims=True)[slots : slots + nearby]

    ones = jnp.ones((8, total_rows), F32)
    for padded, values in ((pose, pose_in), (pmean, pmean_in), (psq, psq_in)):
        padded[...] = ones
        padded[:, 0:pairs] = values[...]
    wide[...] = jnp.zeros_like(wide)
    wide[0:8, :] = pose[...]
    wide[8:16, :] = pmean[...]
    wide[16:24, :] = psq[...]
    wide[24:25, 0:pair_lanes] = local
    details = dot_exact(pick_hot[...], jnp.transpose(wide[:, 0:pair_lanes]))[0:slots]
    wide[...] = jnp.zeros_like(wide)

    def halves(values):
        return values[0:regions] + pltpu.roll(values[regions:slots], 64, 1)

    def from_halves(values):
        low = lax.broadcasted_iota(jnp.int32, values.shape, 1) < 64
        return jnp.concatenate([jnp.where(low, values, 0.0), jnp.where(low, pltpu.roll(values, 64, 1), 0.0)], 0)

    small_out[...] = halves(details)
    small_in[regions - 1 : regions, :] = jnp.ones((1, 128), F32)
    bulk_in[MSG * (regions - 1) : MSG * regions, :] = jnp.zeros((MSG, 128), F32)
    first_in[regions - 1 : regions, :] = jnp.zeros((1, 128), F32)
    for it in range(ITERS):
        second_in[it, regions - 1 : regions, :] = jnp.zeros((1, 128), F32)
    weights = 2.0 * (1.0 + flags.astype(F32))
    weights = jnp.where(real, weights, 0.0)
    weight_column = as_column(weights)
    slot_weights = jnp.sum(jnp.where(picked, weights, 0.0), axis=1, keepdims=True)
    xs[...] = jnp.zeros_like(xs)
    cw[...] = jnp.zeros_like(cw)
    for m in range(MAPS):
        source = points[3 + m] if m < 3 else conf[1]
        chosen = dot(pick_hot[:, 0:pairs], source)
        if m == 3:
            chosen = chosen * slot_weights
        for c in range(CAP):
            for g in range(regions // 8):
                rows = slice(c * regions + 8 * g, c * regions + 8 * g + 8)
                for t in range(TILES):
                    at = MSG * 8 * g + CAP * MAPS * t + MAPS * c + m
                    bulk_out[pl.ds(at, 8, stride=MSG), :] = chosen[rows, 128 * t : 128 * t + 128]
        if m < 3:
            xs[m, near_at:pair_lanes, :] = chosen[slots : slots + nearby]
        else:
            cw[near_at:pair_lanes, :] = chosen[slots : slots + nearby]

    def send_row(src, dst, which, j, to):
        at = pl.ds(j - 1, 1)
        pltpu.make_async_remote_copy(
            src_ref=src.at[at],
            dst_ref=dst.at[at],
            send_sem=send_sem.at[which],
            recv_sem=recv_sem.at[which],
            device_id={"region": to},
        ).start()

    def wait_rows(sem, which, count):
        whole = bulk_in.at[pl.ds(0, count)]
        pltpu.make_async_copy(whole, whole, sem.at[which]).wait()

    pl.semaphore_wait(barrier, regions - 1 + lanes - 1 + jnp.where(lane == 0, 0, 1))

    def send_small(j, carry):
        send_row(small_out, small_in, 0, j, ahead(j))
        return carry

    lax.fori_loop(1, regions, send_small, 0)
    chunk = MSG // CHUNKS
    for h in range(CHUNKS):

        def send_chunk(j, carry, h=h):
            at = pl.ds(pl.multiple_of((j - 1) * MSG + h * chunk, 8), chunk)
            pltpu.make_async_remote_copy(
                src_ref=bulk_out.at[at],
                dst_ref=bulk_in.at[at],
                send_sem=send_sem.at[1 + h],
                recv_sem=recv_sem.at[1 + h],
                device_id={"region": ahead(j)},
            ).start()
            return carry

        def send_both(j, carry, send_chunk=send_chunk):
            return send_chunk(regions - j, send_chunk(j, carry))

        lax.fori_loop(1, regions // 2, send_both, 0)
        send_chunk(regions // 2, 0)

    for m in range(3):
        xs[m, 0:pairs, :] = points[m].astype(F32)
    cw[0:pairs, :] = conf[0].astype(F32) * weight_column[0:pairs]
    def one_hots(column, count):
        key_ids = lax.broadcasted_iota(jnp.int32, (count, gather_hot.shape[1]), 1)
        for n in (2, 1):
            key_ids = jnp.where(key_ids >= n * keys, jnp.where(key_ids < 3 * keys, key_ids - n * keys, -1), key_ids)
        return jnp.where(column == key_ids.astype(F32), 1.0, 0.0)

    hot = one_hots(jnp.concatenate([as_column(firsts)[0:near_at], near], 0), pair_lanes)
    gather_hot[0:pair_lanes, :] = hot.astype(BF16)
    scatter_hot[:, 0:pair_lanes] = jnp.transpose(hot[:, 0:128]).astype(BF16)
    place_ids = lax.broadcasted_iota(jnp.int32, back_hot.shape, 1).astype(F32)
    back_hot[...] = jnp.where(as_column(place) == place_ids, 1.0, 0.0).astype(BF16)

    column_ids = lax.broadcasted_iota(jnp.int32, (8, 128), 1)
    down_step = 8.0 * (128 // ANCH_W)
    row_ids = lax.broadcasted_iota(jnp.int32, (128, 128), 0)
    anchor = lax.broadcasted_iota(jnp.int32, (128, 128), 1)
    anchor_row = lax.div(anchor, jnp.full_like(anchor, ANCH_W))
    across = (8 * (anchor - anchor_row * ANCH_W) + 4 - 4 * ANCH_W).astype(F32)
    downward = (8 * anchor_row + 4 - 4 * ANCH_H).astype(F32)
    kind = lax.rem(row_ids, jnp.full_like(row_ids, COEFS))
    kind = jnp.where(row_ids < 3 * COEFS, kind, -1)
    for k in range(3):
        ray = jnp.where(kind == 4 * k, across, jnp.where(kind == 4 * k + 1, downward, jnp.where(kind == 4 * k + 2, 1.0, 0.0)))
        step = jnp.where(kind == 4 * k + 1, down_step, 0.0)
        move = jnp.where(kind == 4 * k + 3, 1.0, 0.0)
        for b, value in ((k, ray), (3 + k, step), (6 + k, move)):
            camera_ones[:, 128 * b : 128 * b + 128] = value.astype(BF16)
        for j in range(4):
            b = 4 * k + j
            pose_ones[:, 128 * b : 128 * b + 128] = jnp.where(kind == b, 1.0, 0.0).astype(BF16)
    across = across[0:8, :]
    downward = downward[0:8, :]

    for padded, values in ((cam, cam_in), (cmean, cmean_in), (csq, csq_in)):
        padded[...] = jnp.ones((8, 128), F32)
        padded[:, 0:own] = values[...]
    narrow[...] = jnp.zeros_like(narrow)
    rows_g[...] = jnp.zeros_like(rows_g)
    rows_s[...] = jnp.zeros_like(rows_s)
    table[...] = jnp.zeros_like(table)
    small_table[...] = jnp.zeros_like(small_table)

    counter = iter(range(small_send.shape[0]))

    def small_copy(src, dst, device_id):
        which = next(counter)
        return pltpu.make_async_remote_copy(
            src_ref=src,
            dst_ref=dst,
            send_sem=small_send.at[which],
            recv_sem=small_recv.at[which],
            device_id=device_id,
        )

    def fill(ref, at, values):
        for n, piece in enumerate(split_three(values)):
            ref[n * keys + at : n * keys + at + values.shape[0], 0 : values.shape[1]] = piece

    def gather_depths(at, count, begin=0, end=ANCH):
        for n in range(begin, end, 256):
            rows_d[at : at + count, n : n + 256] = dot(gather_hot[at : at + count, :], table[:, n : n + 256])

    def gather_cameras(at, count):
        values = dot(gather_hot[at : at + count, :], small_table[...])
        rows_c[at : at + count, :] = dot(pack_three(values), camera_ones[...])

    def pose_rows(at, values):
        rows_p[at : at + values.shape[0], :] = dot(pack_three(values), pose_ones[...])

    def group(g, inner, begin=0, end=TILES):
        at = pl.ds(pl.multiple_of(g * 8, 8), 8)

        def block(ref, b):
            return ref[at, 128 * b : 128 * b + 128]

        shift = [[block(rows_p, 4 * k + j) for j in range(4)] for k in range(3)]
        ray = [block(rows_c, k) for k in range(3)]
        if begin > 0:
            ray = [ray[k] + F32(begin) * block(rows_c, 3 + k) for k in range(3)]
        zero = jnp.zeros((8, 128), F32)
        turned = [[zero for j in range(3)] for k in range(3)]
        total = [zero for k in range(3)]
        by_depth = [zero for k in range(3)]
        by_down = [zero for k in range(3)]
        for t in range(begin, end):
            part = slice(128 * t, 128 * t + 128)
            d = rows_d[at, part]
            c = cw[at, part]
            x = [xs[j, at, part] for j in range(3)]
            along = None
            for k in range(3):
                placed = shift[k][0] * x[0] + shift[k][1] * x[1] + (shift[k][2] * x[2] + shift[k][3])
                pull = c * ((d * ray[k] + block(rows_c, 6 + k)) - placed)
                for j in range(3):
                    turned[k][j] = turned[k][j] + pull * x[j]
                total[k] = total[k] + pull
                deep = pull * d
                by_depth[k] = by_depth[k] + deep
                if t > 0:
                    by_down[k] = by_down[k] + F32(t) * deep
                along = deep * ray[k] if along is None else along + deep * ray[k]
                if t < end - 1:
                    ray[k] = ray[k] + block(rows_c, 3 + k)
            rows_g[at, part] = along
        out = zero
        for k in range(3):
            values = [by_depth[k] * across, by_depth[k] * downward + by_down[k] * down_step, by_depth[k], total[k]]
            for j in range(4):
                out = jnp.where(column_ids == 4 * k + j, jnp.sum(values[j], axis=1, keepdims=True), out)
            for j in range(3):
                column = COEFS + 4 * k + j
                out = jnp.where(column_ids == column, jnp.sum(turned[k][j], axis=1, keepdims=True), out)
        rows_s[at, :] = out if begin == 0 else rows_s[at, :] + out
        return inner

    def groups(at, count, begin=0, end=TILES):
        lax.fori_loop(at // 8, (at + count) // 8, functools.partial(group, begin=begin, end=end), 0)

    def scatter(rows, keys_from, keys_to, begin=0, end=ANCH):
        hot = scatter_hot[keys_from:keys_to, rows]
        for n in range(begin, end, 256):
            high, low = split_two(rows_g[rows, n : n + 256])
            yield slice(n, n + 256), dot(hot, high) + dot(hot, low)

    def camera_parts():
        q = [cam[k : k + 1, :] for k in range(4)]
        turn, turn_inverse = rotation_rows(*q)
        return q, turn, turn_inverse, jnp.exp(-cam[7:8, :])

    def camera_coefs(it):
        q, turn, turn_inverse, near_focal = camera_parts()
        for k in range(3):
            narrow[4 * k : 4 * k + 1, :] = turn[k][0] * near_focal
            narrow[4 * k + 1 : 4 * k + 2, :] = turn[k][1] * near_focal
            narrow[4 * k + 2 : 4 * k + 3, :] = turn[k][2]
            narrow[4 * k + 3 : 4 * k + 4, :] = cam[4 + k : 5 + k, :]
        coefs = jnp.transpose(narrow[...])[0:own, :]
        edge_c[it, 0] = coefs[0:EDGE, :]
        copy = small_copy(edge_c.at[it, 0], edge_c.at[it, 1], {"region": behind(1)})
        copy.start()
        fill(small_table, 0, coefs)
        return copy

    def pair_coefs():
        p = [pose[k : k + 1, :] for k in range(4)]
        bend, bend_inverse = rotation_rows(*p)
        scale = jnp.exp(pose[7:8, :])
        for k in range(3):
            for j in range(3):
                wide[4 * k + j : 4 * k + j + 1, :] = scale * bend[k][j]
            wide[4 * k + 3 : 4 * k + 4, :] = scale * pose[4 + k : 5 + k, :]
        return jnp.transpose(wide[...])

    def pair_rows(with_slots):
        values = pair_coefs()
        near_values = dot_exact(pick_hot[slots : slots + nearby, :], values[0:pair_lanes])
        values = [values[0:near_at], near_values] + ([values[pair_lanes : pair_lanes + slots]] if with_slots else [])
        pose_rows(0, jnp.concatenate(values, 0))

    def depths(it):
        depth = jnp.exp(logd[it])
        edge_d[it, 0] = depth[0:EDGE, :]
        copy = small_copy(edge_d.at[it, 0], edge_d.at[it, 1], {"region": behind(1)})
        copy.start()
        fill(table, 0, depth)
        return copy

    def edge_rows(it, copies):
        for copy in copies:
            copy.wait_recv()
        blank = jnp.zeros((8, ANCH), F32)
        fill(table, own, jnp.concatenate([edge_d[it, 1], blank], 0))
        fill(small_table, own, jnp.concatenate([edge_c[it, 1], blank[:, 0:128]], 0))
        gather_depths(near_at, nearby)
        gather_cameras(near_at, nearby)
        groups(near_at, nearby)

    def send_edges_back(it):
        back_d[it] = grad_d[own : own + EDGE, :]
        back_c[it, 0] = grad_s[own : own + EDGE, :]
        which = next(counter)
        to_owner = pltpu.make_async_remote_copy(
            src_ref=back_d.at[it],
            dst_ref=part_e.at[it, lane],
            send_sem=small_send.at[which],
            recv_sem=small_recv.at[which],
            device_id={"region": ahead(1), "pair": 0},
        )
        copies = [to_owner, small_copy(back_c.at[it, 0], back_c.at[it, 1], {"region": ahead(1)})]
        for copy in copies:
            copy.start()
        return copies, which

    def take_edges(it, which):
        @pl.when(lane == 0)
        def _():
            whole = part_e.at[it]
            pltpu.make_async_copy(whole, whole, small_recv.at[which]).wait()
            total = part_e[it, 0]
            for k in range(1, lanes):
                total = total + part_e[it, k]
            grad_d[0:EDGE, :] = grad_d[0:EDGE, :] + total

    def send_shares(it, begin, end):
        copies = []
        for k in range(1, lanes):
            to = lane_at(k)
            rows = pl.ds(pl.multiple_of(to * share, share), share)
            columns = pl.ds(begin, end - begin)
            copies.append(small_copy(grad_d.at[rows, columns], part_d.at[it, k - 1, :, columns], {"pair": to}))
        for copy in copies:
            copy.start()
        return copies

    def update_depths(it, begin, end, copies):
        for copy in copies:
            copy.wait_recv()
        columns = slice(begin, end)
        gradient = grad_d[pl.ds(my_rows, share), columns]
        for k in range(1, lanes):
            gradient = gradient + part_d[it, k - 1, :, columns]
        updated, dmean[:, columns], dsq[:, columns] = adam(
            logd[it, pl.ds(my_rows, share), columns], gradient, dmean[:, columns], dsq[:, columns], it
        )
        logd[it + 1, pl.ds(my_rows, share), columns] = updated
        mine = logd.at[it + 1, pl.ds(my_rows, share), pl.ds(begin, end - begin)]
        gathers = [small_copy(mine, mine, {"pair": lane_at(k)}) for k in range(1, lanes)]
        for copy in gathers:
            copy.start()
        return gathers

    def send_cameras(it, sums, back_copy):
        back_copy.wait_recv()
        sums = jnp.concatenate([sums[0:EDGE, :] + back_c[it, 1], sums[EDGE:own, :]], 0)
        if own < 128:
            sums = jnp.concatenate([sums, jnp.zeros((128 - own, 128), F32)], 0)
        part_c[it, lane] = jnp.transpose(sums)[0:16, :]
        copies = [small_copy(part_c.at[it, lane], part_c.at[it, lane], {"pair": lane_at(k)}) for k in range(1, lanes)]
        for copy in copies:
            copy.start()
        return copies

    def update_cameras(it, copies):
        for copy in copies:
            copy.wait_recv()
        q, turn, turn_inverse, near_focal = camera_parts()
        found = part_c[it, 0]
        for k in range(1, lanes):
            found = found + part_c[it, k]
        across_sum = [found[4 * k : 4 * k + 1, :] * near_focal for k in range(3)]
        down_sum = [found[4 * k + 1 : 4 * k + 2, :] * near_focal for k in range(3)]
        g_turn = [[across_sum[k], down_sum[k], found[4 * k + 2 : 4 * k + 3, :]] for k in range(3)]
        g_cam = rotation_pull(q, turn, turn_inverse, g_turn)
        for k in range(3):
            g_cam.append(found[4 * k + 3 : 4 * k + 4, :])
        g_cam.append(-sum(turn[k][0] * across_sum[k] + turn[k][1] * down_sum[k] for k in range(3)))
        for k in range(8):
            row = slice(k, k + 1)
            cam[row, :], cmean[row, :], csq[row, :] = adam(cam[row, :], g_cam[k], cmean[row, :], csq[row, :], it)

    def send_sums(it):
        second_out[it] = halves(rows_s[pair_lanes : pair_lanes + slots, :])

        def send(j, inner):
            send_row(second_out.at[it], second_in.at[it], 2 + CHUNKS + it, j, behind(j))
            return inner

        lax.fori_loop(1, regions, send, 0)

    def update_pairs(it, with_slots):
        wait_rows(recv_sem, 2 + CHUNKS + it, regions - 1)
        seconds = jnp.concatenate([from_halves(second_in[it]), rows_s[near_at:pair_lanes, :]], 0)
        of_pairs = dot_exact(back_hot[...], seconds)
        found = [of_pairs[0:near_at] + rows_s[0:near_at, :], of_pairs[near_at:pair_lanes]]
        if with_slots:
            wait_rows(recv_sem, 1 + CHUNKS, regions - 1)
            found.append(from_halves(first_in[...]) + rows_s[pair_lanes : pair_lanes + slots, :])
            if slots < total_rows - pair_lanes:
                found.append(jnp.zeros((total_rows - pair_lanes - slots, 128), F32))
        found = jnp.transpose(jnp.concatenate(found, 0))
        lanes_used = slice(0, total_rows if with_slots else pair_lanes)
        m = [[found[COEFS + 4 * k + j : COEFS + 4 * k + j + 1, :] for j in range(3)] for k in range(3)]
        v = [found[4 * k + 3 : 4 * k + 4, :] for k in range(3)]
        p = [pose[k : k + 1, lanes_used] for k in range(4)]
        bend, bend_inverse = rotation_rows(*p)
        scale = jnp.exp(pose[7:8, lanes_used])
        g_turn = [[-(scale * m[k][j]) for j in range(3)] for k in range(3)]
        g_pose = rotation_pull(p, bend, bend_inverse, g_turn)
        g_scale = sum(bend[k][j] * g_turn[k][j] for k in range(3) for j in range(3))
        for k in range(3):
            g_move = -(scale * v[k])
            g_scale = g_scale + pose[4 + k : 5 + k, lanes_used] * g_move
            g_pose.append(g_move)
        g_pose.append(g_scale)
        for k in range(8):
            row = (slice(k, k + 1), lanes_used)
            pose[row], pmean[row], psq[row] = adam(pose[row], g_pose[k], pmean[row], psq[row], it)

    near_side = slice(0, pair_lanes)
    far_side = slice(pair_lanes, total_rows)
    sent = []

    edges = [camera_coefs(0), depths(0)]
    sent += edges
    gather_depths(0, near_at)
    gather_cameras(0, near_at)
    pair_rows(False)
    groups(0, near_at)
    first_out[...] = halves(dot_exact(pick_hot[0:slots, :], rows_s[0:pair_lanes, :]))

    def send_first(j, inner):
        send_row(first_out, first_in, 1 + CHUNKS, j, ahead(j))
        return inner

    lax.fori_loop(1, regions, send_first, 0)
    edge_rows(0, edges)
    for part, value in scatter(near_side, 0, keys):
        grad_d[:, part] = value
    grad_s[...] = dot_exact(scatter_hot[0:keys, near_side], rows_s[near_side, :])
    back, edge_sem = send_edges_back(0)
    sent += back
    wait_rows(recv_sem, 0, regions - 1)
    named = from_halves(small_in[...])
    hot = one_hots(named[:, 24:25], slots)
    gather_hot[pair_lanes : pair_lanes + slots, :] = hot.astype(BF16)
    if slots < 128:
        hot = jnp.concatenate([hot, jnp.zeros((128 - slots, hot.shape[1]), F32)], 0)
        named = jnp.concatenate([named, jnp.ones((128 - slots, 128), F32)], 0)
    scatter_hot[:, far_side] = jnp.transpose(hot[:, 0:128]).astype(BF16)
    named = jnp.transpose(named)
    pose[:, far_side] = named[0:8, :]
    pmean[:, far_side] = named[8:16, :]
    psq[:, far_side] = named[16:24, :]
    pose_rows(pair_lanes, pair_coefs()[pair_lanes : pair_lanes + slots])
    gather_cameras(pair_lanes, slots)
    gather_depths(pair_lanes, slots)
    take_edges(0, edge_sem)
    gathers = []
    shared = []
    pending = None
    tiles = TILES // CHUNKS
    for h in range(CHUNKS):
        wait_rows(recv_sem, 1 + h, chunk * (regions - 1))
        begin, end = 128 * tiles * h, 128 * tiles * (h + 1)
        for c in range(CAP):
            for g in range(regions // 8):
                at = pair_lanes + c * regions + 8 * g
                for t in range(tiles * h, tiles * (h + 1)):
                    for m in range(MAPS):
                        source = MSG * 8 * g + CAP * MAPS * t + MAPS * c + m
                        value = bulk_in[pl.ds(source, 8, stride=MSG), :]
                        if m < 3:
                            xs[m, at : at + 8, 128 * t : 128 * t + 128] = value
                        else:
                            cw[at : at + 8, 128 * t : 128 * t + 128] = value
        groups(pair_lanes, slots, tiles * h, tiles * (h + 1))
        for part, value in scatter(far_side, 0, own, begin, end):
            grad_d[0:own, part] = grad_d[0:own, part] + value
        shares = send_shares(0, begin, end)
        shared += shares
        if pending is not None:
            gathers += update_depths(0, *pending)
        pending = (begin, end, shares)
    sums = grad_s[0:own, :] + dot_exact(scatter_hot[0:own, far_side], rows_s[far_side, :])
    cameras = send_cameras(0, sums, back[1])
    sent += cameras
    send_sums(0)
    gathers += update_depths(0, *pending)
    update_cameras(0, cameras)
    edges = [camera_coefs(1)]
    gather_cameras(0, near_at)
    gather_cameras(pair_lanes, slots)
    update_pairs(0, True)
    pair_rows(True)

    for copy in gathers:
        copy.wait_recv()
    sent += gathers
    edges.append(depths(1))
    sent += edges
    gather_depths(0, near_at)
    gather_depths(pair_lanes, slots)
    groups(0, near_at)
    groups(pair_lanes, slots)
    edge_rows(1, edges)
    for copy in shared:
        copy.wait_send()
    rows = slice(0, total_rows)
    for part, value in scatter(rows, 0, keys):
        grad_d[:, part] = value
    shares = send_shares(1, 0, ANCH)
    grad_s[...] = dot_exact(scatter_hot[0:keys, rows], rows_s[rows, :])
    back, edge_sem = send_edges_back(1)
    send_sums(1)
    cameras = send_cameras(1, grad_s[0:own, :], back[1])
    take_edges(1, edge_sem)
    gathers = update_depths(1, 0, ANCH, shares)
    sent += shares + back + cameras
    update_cameras(1, cameras)
    update_pairs(1, False)

    wait_rows(send_sem, 0, regions - 1)
    for h in range(CHUNKS):
        wait_rows(send_sem, 1 + h, chunk * (regions - 1))
    for n in range(1 + ITERS):
        wait_rows(send_sem, 1 + CHUNKS + n, regions - 1)
    for copy in sent:
        copy.wait_send()
    cam_in[...] = cam[:, 0:own]
    pose_in[...] = pose[:, 0:pairs]
    pmean_in[...] = pmean[:, 0:pairs]
    psq_in[...] = psq[:, 0:pairs]
    for n, src in enumerate((cmean, csq)):
        value = src[:, 0:share]
        for k in range(1, lanes):
            value = jnp.where(lane == k, src[:, k * share : (k + 1) * share], value)
        moments[n] = value
    stores = [
        pltpu.make_async_copy(src, dst, load_sem.at[n])
        for n, (src, dst) in enumerate(
            (
                (logd.at[ITERS], logd_out), (cam_in, cam_out), (pose_in, pose_out), (dmean, dmean_out), (dsq, dsq_out),
                (moments.at[0], cmean_out), (moments.at[1], csq_out), (pmean_in, pmean_out), (psq_in, psq_out),
            )
        )
    ]
    for store in stores[1:]:
        store.start()
    for copy in gathers:
        copy.wait()
    stores[0].start()
    for store in stores:
        store.wait()


def deliver(*refs):
    sources, results, held, sems = refs[0:9], refs[9:18], refs[18:27], refs[27]
    for bring in (True, False):
        copies = [
            pltpu.make_async_copy(sources[n] if bring else held[n], held[n] if bring else results[n], sems.at[n])
            for n in range(9)
        ]
        for copy in copies:
            copy.start()
        for copy in copies:
            copy.wait()


def shards(
    log_depth, cameras, pair_pose, depth_mean, depth_square, camera_mean, camera_square, pose_mean, pose_square,
    pointmaps, confidence, pair_images, pair_flag,
):
    regions = lax.axis_size("region")
    lanes = lax.axis_size("pair")
    own = log_depth.shape[0]
    pairs = pair_pose.shape[0]
    share = own // lanes
    slots = CAP * regions
    nearby = pairs - CAP * (regions - 1)
    pair_lanes = rounded(pairs, 128)
    total_rows = pair_lanes + rounded(slots, 128)
    keys = own + 16
    key_lanes = rounded(3 * keys, 128)
    in_hbm = pl.BlockSpec(memory_space=pltpu.HBM)

    def vmem(*shape, dtype=F32):
        return pltpu.VMEM(shape, dtype)

    def out(*shape):
        return jax.ShapeDtypeStruct(shape, F32)

    shapes = (
        out(own, ANCH), out(8, own), out(8, pairs), out(share, ANCH), out(share, ANCH),
        out(8, share), out(8, share), out(8, pairs), out(8, pairs),
    )
    results = pl.pallas_call(
        functools.partial(kernel, regions, lanes, own, pairs),
        out_shape=shapes,
        in_specs=[in_hbm] * 13,
        out_specs=(in_hbm,) * 9,
        scratch_shapes=[
            vmem(8, own), vmem(8, own), vmem(8, own), vmem(8, pairs), vmem(8, pairs), vmem(8, pairs),
            vmem(2, pairs, dtype=jnp.int32), vmem(1, pairs, dtype=jnp.int32),
            vmem(ITERS + 1, own, ANCH), vmem(share, ANCH), vmem(share, ANCH),
            vmem(8, 128), vmem(8, 128), vmem(8, 128),
            vmem(8, total_rows), vmem(8, total_rows), vmem(8, total_rows),
            vmem(6, pairs, ANCH, dtype=BF16), vmem(2, pairs, ANCH, dtype=BF16),
            vmem(3, total_rows, ANCH), vmem(total_rows, ANCH),
            vmem(8, pair_lanes, dtype=jnp.int32),
            vmem(slots + nearby, pair_lanes, dtype=BF16), vmem(pair_lanes, slots + nearby, dtype=BF16),
            vmem(total_rows, key_lanes, dtype=BF16), vmem(128, total_rows, dtype=BF16),
            vmem(128, 9 * 128, dtype=BF16), vmem(128, 12 * 128, dtype=BF16),
            vmem(key_lanes, ANCH, dtype=BF16), vmem(key_lanes, 128, dtype=BF16),
            vmem(total_rows, ANCH), vmem(total_rows, 9 * 128), vmem(total_rows, 12 * 128),
            vmem(total_rows, ANCH), vmem(total_rows, 128),
            vmem(128, total_rows), vmem(128, 128), vmem(keys, ANCH), vmem(keys, 128),
            vmem(regions, 128), vmem(regions, 128), vmem(MSG * regions, 128), vmem(MSG * regions, 128),
            vmem(regions, 128), vmem(regions, 128), vmem(ITERS, regions, 128), vmem(ITERS, regions, 128),
            vmem(ITERS, 2, EDGE, ANCH), vmem(ITERS, 2, EDGE, 128),
            vmem(ITERS, EDGE, ANCH), vmem(ITERS, 2, EDGE, 128),
            vmem(ITERS, lanes - 1, share, ANCH), vmem(ITERS, lanes, EDGE, ANCH), vmem(ITERS, lanes, 16, 128), vmem(2, 8, share),
            pltpu.SemaphoreType.DMA((13,)),
            pltpu.SemaphoreType.DMA((2 + CHUNKS + ITERS,)), pltpu.SemaphoreType.DMA((2 + CHUNKS + ITERS,)),
            pltpu.SemaphoreType.DMA((48,)), pltpu.SemaphoreType.DMA((48,)),
        ],
        compiler_params=pltpu.CompilerParams(
            collective_id=0, has_side_effects=True, vmem_limit_bytes=62 * 1024 * 1024
        ),
        name="align",
    )(
        log_depth, cameras.T, pair_pose.T, depth_mean, depth_square, camera_mean.T, camera_square.T,
        pose_mean.T, pose_square.T, pointmaps.transpose(1, 0, 2), confidence.transpose(1, 0, 2),
        pair_images.T, pair_flag.reshape(1, pairs),
    )
    depth, camera, pose, dmean, dsq, cmean, csq, pmean, psq = pl.pallas_call(
        deliver,
        out_shape=shapes,
        in_specs=[in_hbm] * 9,
        out_specs=(in_hbm,) * 9,
        scratch_shapes=[vmem(*shape.shape) for shape in shapes] + [pltpu.SemaphoreType.DMA((9,))],
        compiler_params=pltpu.CompilerParams(vmem_limit_bytes=62 * 1024 * 1024),
        name="deliver",
    )(*results)
    return depth, camera.T, pose.T, dmean, dsq, cmean.T, csq.T, pmean.T, psq.T


def solution(mesh):
    placed = (
        P("region", None),
        P("region", None),
        P(("region", "pair"), None),
        P("region", None),
        P("region", None),
        P("region", None),
        P("region", None),
        P(("region", "pair"), None),
        P(("region", "pair"), None),
        P(("region", "pair"), None, None),
        P(("region", "pair"), None, None),
        P(("region", "pair"), None),
        P(("region", "pair")),
    )
    return jax.shard_map(
        shards,
        mesh=mesh,
        in_specs=placed,
        out_specs=(
            P("region", None),
            P("region", None),
            P(("region", "pair"), None),
            P(("region", "pair"), None),
            P(("region", "pair"), None),
            P(("region", "pair"), None),
            P(("region", "pair"), None),
            P(("region", "pair"), None),
            P(("region", "pair"), None),
        ),
        check_vma=False,
    )
```

```python
import functools

import jax
import jax.numpy as jnp
from jax import lax
from jax.experimental import pallas as pl
from jax.experimental.pallas import tpu as pltpu
from jax.sharding import PartitionSpec as P

ANCH_W = 32
ANCH_H = 24
ANCH = 768
CAP = 2
NEIGHBOURS = 4
ITERS = 2
START = 300

LEARN_RATE = 0.01
BETA_ONE = 0.9
BETA_TWO = 0.999
EPSILON = 1e-08

TILES = ANCH // 128
EDGE = 8
MAPS = 4
MSG = TILES * CAP * MAPS
CHUNKS = 3
COEFS = 16
F32 = jnp.float32
BF16 = jnp.bfloat16


def rounded(value, multiple):
    return -(-value // multiple) * multiple


def split_two(x):
    high = x.astype(BF16)
    return high, (x - high.astype(F32)).astype(BF16)


def split_three(x):
    high = x.astype(BF16)
    rest = x - high.astype(F32)
    middle = rest.astype(BF16)
    return high, middle, (rest - middle.astype(F32)).astype(BF16)


def dot(a, b):
    return jnp.dot(a, b, preferred_element_type=F32)


def dot_exact(one_hot, x):
    high, middle, low = split_three(x)
    return dot(one_hot, high) + (dot(one_hot, middle) + dot(one_hot, low))


def pack_three(x):
    high, middle, low = split_three(x)
    rest = pltpu.roll(middle.astype(F32), COEFS, 1) + pltpu.roll(low.astype(F32), 2 * COEFS, 1)
    return (high.astype(F32) + rest).astype(BF16)


def rotation_rows(w, x, y, z):
    inverse = 1.0 / (w * w + x * x + y * y + z * z)
    matrix = [
        [w * w + x * x - y * y - z * z, 2.0 * (x * y - w * z), 2.0 * (x * z + w * y)],
        [2.0 * (x * y + w * z), w * w - x * x + y * y - z * z, 2.0 * (y * z - w * x)],
        [2.0 * (x * z - w * y), 2.0 * (y * z + w * x), w * w - x * x - y * y + z * z],
    ]
    return [[entry * inverse for entry in line] for line in matrix], inverse


def rotation_pull(q, matrix, inverse, g):
    w, x, y, z = q
    along = sum(g[k][j] * matrix[k][j] for k in range(3) for j in range(3))
    diag = g[0][0] + g[1][1] + g[2][2]
    g_w = w * diag + z * (g[1][0] - g[0][1]) + y * (g[0][2] - g[2][0]) + x * (g[2][1] - g[1][2])
    g_x = (
        x * (g[0][0] - g[1][1] - g[2][2])
        + y * (g[0][1] + g[1][0])
        + z * (g[0][2] + g[2][0])
        + w * (g[2][1] - g[1][2])
    )
    g_y = (
        y * (g[1][1] - g[0][0] - g[2][2])
        + x * (g[0][1] + g[1][0])
        + z * (g[1][2] + g[2][1])
        + w * (g[0][2] - g[2][0])
    )
    g_z = (
        z * (g[2][2] - g[0][0] - g[1][1])
        + x * (g[0][2] + g[2][0])
        + y * (g[1][2] + g[2][1])
        + w * (g[1][0] - g[0][1])
    )
    twice = 2.0 * inverse
    return [twice * (g_w - w * along), twice * (g_x - x * along), twice * (g_y - y * along), twice * (g_z - z * along)]


def adam(param, gradient, mean, square, it):
    fix_one = 1.0 - BETA_ONE ** (START + 1 + it)
    fix_two = 1.0 - BETA_TWO ** (START + 1 + it)
    mean = BETA_ONE * mean + (1.0 - BETA_ONE) * gradient
    square = BETA_TWO * square + (1.0 - BETA_TWO) * gradient * gradient
    param = param - LEARN_RATE * (mean / fix_one) / (jnp.sqrt(square / fix_two) + EPSILON)
    return param, mean, square


def kernel(
    regions, lanes, own, pairs,
    logd_hbm, cam_hbm, pose_hbm, dmean_hbm, dsq_hbm, cmean_hbm, csq_hbm, pmean_hbm, psq_hbm, points_hbm, conf_hbm,
    images_hbm, flag_hbm,
    logd_out, cam_out, pose_out, dmean_out, dsq_out, cmean_out, csq_out, pmean_out, psq_out,
    cam_in, cmean_in, csq_in, pose_in, pmean_in, psq_in, images_in, flag_in,
    logd, dmean, dsq, cam, cmean, csq, pose, pmean, psq, points, conf, xs, cw,
    index_rows, pick_hot, back_hot, gather_hot, scatter_hot, camera_ones, pose_ones,
    table, small_table, rows_d, rows_c, rows_p, rows_g, rows_s, wide, narrow, grad_d, grad_s,
    small_out, small_in, bulk_out, bulk_in, first_out, first_in, second_out, second_in,
    edge_d, edge_c, back_d, back_c, part_d, part_e, part_c, moments,
    load_sem, send_sem, recv_sem, small_send, small_recv,
):
    share = own // lanes
    slots = CAP * regions
    nearby = pairs - CAP * (regions - 1)
    pair_lanes = pose.shape[1] - rounded(slots, 128)
    total_rows = pose.shape[1]
    near_at = pair_lanes - nearby
    keys = own + 16
    region = lax.axis_index("region")
    lane = lax.axis_index("pair")
    my_rows = pl.multiple_of(lane * share, share)

    def ahead(j):
        return lax.rem(region + j, regions)

    def behind(j):
        return lax.rem(region - j + regions, regions)

    def lane_at(k):
        return lax.rem(lane + k, lanes)

    loads = [
        pltpu.make_async_copy(src, dst, load_sem.at[n])
        for n, (src, dst) in enumerate(
            (
                (images_hbm, images_in), (flag_hbm, flag_in), (points_hbm, points), (conf_hbm, conf), (logd_hbm, logd.at[0]),
                (cam_hbm, cam_in), (cmean_hbm, cmean_in), (csq_hbm, csq_in),
                (pose_hbm, pose_in), (pmean_hbm, pmean_in), (psq_hbm, psq_in),
                (dmean_hbm.at[pl.ds(my_rows, share)], dmean), (dsq_hbm.at[pl.ds(my_rows, share)], dsq),
            )
        )
    ]
    for load in loads:
        load.start()

    barrier = pltpu.get_barrier_semaphore()

    def greet(j, carry):
        pl.semaphore_signal(barrier, inc=1, device_id={"region": ahead(j)})
        return carry

    lax.fori_loop(1, regions, greet, 0)
    for k in range(1, lanes):
        pl.semaphore_signal(barrier, inc=1, device_id={"pair": lane_at(k)})


    @pl.when(lane == 0)
    def _():
        for k in range(1, lanes):
            pl.semaphore_signal(barrier, inc=1, device_id={"region": behind(1), "pair": k})

    for load in loads:
        load.wait()

    def as_column(row):
        return jnp.transpose(jnp.broadcast_to(row, (128, row.shape[1])))[:, 0:1]

    lane_ids = lax.broadcasted_iota(jnp.int32, (1, pair_lanes), 1)
    index_rows[...] = jnp.zeros_like(index_rows)
    index_rows[0:2, 0:pairs] = images_in[...]
    index_rows[2:3, 0:pairs] = flag_in[...]
    real = lane_ids < pairs
    seconds = index_rows[1:2, :]
    flags = index_rows[2:3, :]
    remote = jnp.logical_and(flags == 1, real)
    firsts = jnp.where(real, index_rows[0:1, :] - region * own, 0).astype(F32)
    target = lax.div(seconds, jnp.full_like(seconds, own))
    local = seconds - target * own
    offset = target - region
    offset = jnp.where(offset < 0, offset + regions, offset)
    offset = jnp.where(remote, offset, 0).astype(F32)
    near = jnp.where(target == region, local, own + local).astype(F32)
    local = local.astype(F32)
    earlier_ids = lax.broadcasted_iota(jnp.int32, (pair_lanes, pair_lanes), 0)
    later_ids = lax.broadcasted_iota(jnp.int32, (pair_lanes, pair_lanes), 1)
    same = jnp.logical_and(as_column(offset) == offset, earlier_ids < later_ids)
    rank = jnp.sum(jnp.where(same, 1.0, 0.0), axis=0, keepdims=True)
    place = jnp.where(remote, rank * regions + offset - 1.0, slots + rank)
    place = jnp.where(real, place, -1.0)
    place_ids = lax.broadcasted_iota(jnp.int32, pick_hot.shape, 0).astype(F32)
    picked = place_ids == place
    pick_hot[...] = jnp.where(picked, 1.0, 0.0).astype(BF16)
    near = jnp.sum(jnp.where(picked, near, 0.0), axis=1, keepdims=True)[slots : slots + nearby]

    ones = jnp.ones((8, total_rows), F32)
    for padded, values in ((pose, pose_in), (pmean, pmean_in), (psq, psq_in)):
        padded[...] = ones
        padded[:, 0:pairs] = values[...]
    wide[...] = jnp.zeros_like(wide)
    wide[0:8, :] = pose[...]
    wide[8:16, :] = pmean[...]
    wide[16:24, :] = psq[...]
    wide[24:25, 0:pair_lanes] = local
    details = dot_exact(pick_hot[...], jnp.transpose(wide[:, 0:pair_lanes]))[0:slots]
    wide[...] = jnp.zeros_like(wide)

    def halves(values):
        return values[0:regions] + pltpu.roll(values[regions:slots], 64, 1)

    def from_halves(values):
        low = lax.broadcasted_iota(jnp.int32, values.shape, 1) < 64
        return jnp.concatenate([jnp.where(low, values, 0.0), jnp.where(low, pltpu.roll(values, 64, 1), 0.0)], 0)

    small_out[...] = halves(details)
    small_in[regions - 1 : regions, :] = jnp.ones((1, 128), F32)
    bulk_in[MSG * (regions - 1) : MSG * regions, :] = jnp.zeros((MSG, 128), F32)
    first_in[regions - 1 : regions, :] = jnp.zeros((1, 128), F32)
    for it in range(ITERS):
        second_in[it, regions - 1 : regions, :] = jnp.zeros((1, 128), F32)
    weights = 2.0 * (1.0 + flags.astype(F32))
    weights = jnp.where(real, weights, 0.0)
    weight_column = as_column(weights)
    slot_weights = jnp.sum(jnp.where(picked, weights, 0.0), axis=1, keepdims=True)
    xs[...] = jnp.zeros_like(xs)
    cw[...] = jnp.zeros_like(cw)
    for m in range(MAPS):
        source = points[3 + m] if m < 3 else conf[:, 1, :]
        chosen = dot(pick_hot[:, 0:pairs], source)
        if m == 3:
            chosen = chosen * slot_weights
        for c in range(CAP):
            for g in range(regions // 8):
                rows = slice(c * regions + 8 * g, c * regions + 8 * g + 8)
                for t in range(TILES):
                    at = MSG * 8 * g + CAP * MAPS * t + MAPS * c + m
                    bulk_out[pl.ds(at, 8, stride=MSG), :] = chosen[rows, 128 * t : 128 * t + 128]
        if m < 3:
            xs[m, near_at:pair_lanes, :] = chosen[slots : slots + nearby]
        else:
            cw[near_at:pair_lanes, :] = chosen[slots : slots + nearby]

    def send_row(src, dst, which, j, to):
        at = pl.ds(j - 1, 1)
        pltpu.make_async_remote_copy(
            src_ref=src.at[at],
            dst_ref=dst.at[at],
            send_sem=send_sem.at[which],
            recv_sem=recv_sem.at[which],
            device_id={"region": to},
        ).start()

    def wait_rows(sem, which, count):
        whole = bulk_in.at[pl.ds(0, count)]
        pltpu.make_async_copy(whole, whole, sem.at[which]).wait()

    def one_hots(column, count):
        key_ids = lax.broadcasted_iota(jnp.int32, (count, gather_hot.shape[1]), 1)
        for n in (2, 1):
            key_ids = jnp.where(key_ids >= n * keys, jnp.where(key_ids < 3 * keys, key_ids - n * keys, -1), key_ids)
        return jnp.where(column == key_ids.astype(F32), 1.0, 0.0)

    column_ids = lax.broadcasted_iota(jnp.int32, (8, 128), 1)
    for padded, values in ((cam, cam_in), (cmean, cmean_in), (csq, csq_in)):
        padded[...] = jnp.ones((8, 128), F32)
        padded[:, 0:own] = values[...]
    narrow[...] = jnp.zeros_like(narrow)
    table[...] = jnp.zeros_like(table)
    small_table[...] = jnp.zeros_like(small_table)

    counter = iter(range(small_send.shape[0]))

    def small_copy(src, dst, device_id):
        which = next(counter)
        return pltpu.make_async_remote_copy(
            src_ref=src,
            dst_ref=dst,
            send_sem=small_send.at[which],
            recv_sem=small_recv.at[which],
            device_id=device_id,
        )

    def fill(ref, at, values):
        for n, piece in enumerate(split_three(values)):
            ref[n * keys + at : n * keys + at + values.shape[0], 0 : values.shape[1]] = piece

    def gather_depths(at, count, begin=0, end=ANCH):
        for n in range(begin, end, 256):
            rows_d[at : at + count, n : n + 256] = dot(gather_hot[at : at + count, :], table[:, n : n + 256])

    def gather_cameras(at, count):
        values = dot(gather_hot[at : at + count, :], small_table[...])
        rows_c[at : at + count, :] = dot(pack_three(values), camera_ones[...])

    def pose_rows(at, values):
        rows_p[at : at + values.shape[0], :] = dot(pack_three(values), pose_ones[...])

    def group(g, inner, begin=0, end=TILES):
        at = pl.ds(pl.multiple_of(g * 8, 8), 8)

        def block(ref, b):
            return ref[at, 128 * b : 128 * b + 128]

        shift = [[block(rows_p, 4 * k + j) for j in range(4)] for k in range(3)]
        ray = [block(rows_c, k) for k in range(3)]
        if begin > 0:
            ray = [ray[k] + F32(begin) * block(rows_c, 3 + k) for k in range(3)]
        zero = jnp.zeros((8, 128), F32)
        turned = [[zero for j in range(3)] for k in range(3)]
        total = [zero for k in range(3)]
        by_depth = [zero for k in range(3)]
        by_down = [zero for k in range(3)]
        for t in range(begin, end):
            part = slice(128 * t, 128 * t + 128)
            d = rows_d[at, part]
            c = cw[at, part]
            x = [xs[j, at, part] for j in range(3)]
            along = None
            for k in range(3):
                placed = shift[k][0] * x[0] + shift[k][1] * x[1] + (shift[k][2] * x[2] + shift[k][3])
                pull = c * ((d * ray[k] + block(rows_c, 6 + k)) - placed)
                for j in range(3):
                    turned[k][j] = turned[k][j] + pull * x[j]
                total[k] = total[k] + pull
                deep = pull * d
                by_depth[k] = by_depth[k] + deep
                if t > 0:
                    by_down[k] = by_down[k] + F32(t) * deep
                along = deep * ray[k] if along is None else along + deep * ray[k]
                if t < end - 1:
                    ray[k] = ray[k] + block(rows_c, 3 + k)
            rows_g[at, part] = along
        out = zero
        for k in range(3):
            values = [by_depth[k] * across, by_depth[k] * downward + by_down[k] * down_step, by_depth[k], total[k]]
            for j in range(4):
                out = jnp.where(column_ids == 4 * k + j, jnp.sum(values[j], axis=1, keepdims=True), out)
            for j in range(3):
                column = COEFS + 4 * k + j
                out = jnp.where(column_ids == column, jnp.sum(turned[k][j], axis=1, keepdims=True), out)
        rows_s[at, :] = out if begin == 0 else rows_s[at, :] + out
        return inner

    def groups(at, count, begin=0, end=TILES):
        lax.fori_loop(at // 8, (at + count) // 8, functools.partial(group, begin=begin, end=end), 0, unroll=4)

    def scatter(rows, keys_from, keys_to, begin=0, end=ANCH):
        hot = scatter_hot[keys_from:keys_to, rows]
        for n in range(begin, end, 256):
            high, low = split_two(rows_g[rows, n : n + 256])
            yield slice(n, n + 256), dot(hot, high) + dot(hot, low)

    def camera_parts():
        q = [cam[k : k + 1, :] for k in range(4)]
        turn, turn_inverse = rotation_rows(*q)
        return q, turn, turn_inverse, jnp.exp(-cam[7:8, :])

    def camera_coefs(it):
        q, turn, turn_inverse, near_focal = camera_parts()
        for k in range(3):
            narrow[4 * k : 4 * k + 1, :] = turn[k][0] * near_focal
            narrow[4 * k + 1 : 4 * k + 2, :] = turn[k][1] * near_focal
            narrow[4 * k + 2 : 4 * k + 3, :] = turn[k][2]
            narrow[4 * k + 3 : 4 * k + 4, :] = cam[4 + k : 5 + k, :]
        coefs = jnp.transpose(narrow[...])[0:own, :]
        edge_c[it, 0] = coefs[0:EDGE, :]
        fill(small_table, 0, coefs)
        return small_copy(edge_c.at[it, 0], edge_c.at[it, 1], {"region": behind(1)})

    def pair_coefs():
        p = [pose[k : k + 1, :] for k in range(4)]
        bend, bend_inverse = rotation_rows(*p)
        scale = jnp.exp(pose[7:8, :])
        for k in range(3):
            for j in range(3):
                wide[4 * k + j : 4 * k + j + 1, :] = scale * bend[k][j]
            wide[4 * k + 3 : 4 * k + 4, :] = scale * pose[4 + k : 5 + k, :]
        return jnp.transpose(wide[...])

    def pair_rows(with_slots):
        values = pair_coefs()
        near_values = dot_exact(pick_hot[slots : slots + nearby, :], values[0:pair_lanes])
        values = [values[0:near_at], near_values] + ([values[pair_lanes : pair_lanes + slots]] if with_slots else [])
        pose_rows(0, jnp.concatenate(values, 0))

    def depths(it):
        depth = jnp.exp(logd[it])
        edge_d[it, 0] = depth[0:EDGE, :]
        copy = small_copy(edge_d.at[it, 0], edge_d.at[it, 1], {"region": behind(1)})
        if it > 0:
            copy.start()
        fill(table, 0, depth)
        return copy

    def edge_rows(it, copies):
        for copy in copies:
            copy.wait_recv()
        blank = jnp.zeros((8, ANCH), F32)
        fill(table, own, jnp.concatenate([edge_d[it, 1], blank], 0))
        fill(small_table, own, jnp.concatenate([edge_c[it, 1], blank[:, 0:128]], 0))
        gather_depths(near_at, nearby)
        gather_cameras(near_at, nearby)
        groups(near_at, nearby)

    def send_edges_back(it):
        back_d[it] = grad_d[own : own + EDGE, :]
        back_c[it, 0] = grad_s[own : own + EDGE, :]
        which = next(counter)
        to_owner = pltpu.make_async_remote_copy(
            src_ref=back_d.at[it],
            dst_ref=part_e.at[it, lane],
            send_sem=small_send.at[which],
            recv_sem=small_recv.at[which],
            device_id={"region": ahead(1), "pair": 0},
        )
        copies = [to_owner, small_copy(back_c.at[it, 0], back_c.at[it, 1], {"region": ahead(1)})]
        for copy in copies:
            copy.start()
        return copies, which

    def take_edges(it, which):
        @pl.when(lane == 0)
        def _():
            whole = part_e.at[it]
            pltpu.make_async_copy(whole, whole, small_recv.at[which]).wait()
            total = part_e[it, 0]
            for k in range(1, lanes):
                total = total + part_e[it, k]
            grad_d[0:EDGE, :] = grad_d[0:EDGE, :] + total

    def send_shares(it, begin, end):
        copies = []
        for k in range(1, lanes):
            to = lane_at(k)
            rows = pl.ds(pl.multiple_of(to * share, share), share)
            columns = pl.ds(begin, end - begin)
            copies.append(small_copy(grad_d.at[rows, columns], part_d.at[it, k - 1, :, columns], {"pair": to}))
        for copy in copies:
            copy.start()
        return copies

    def update_depths(it, begin, end, copies):
        for copy in copies:
            copy.wait_recv()
        columns = slice(begin, end)
        gradient = grad_d[pl.ds(my_rows, share), columns]
        for k in range(1, lanes):
            gradient = gradient + part_d[it, k - 1, :, columns]
        updated, dmean[:, columns], dsq[:, columns] = adam(
            logd[it, pl.ds(my_rows, share), columns], gradient, dmean[:, columns], dsq[:, columns], it
        )
        logd[it + 1, pl.ds(my_rows, share), columns] = updated
        mine = logd.at[it + 1, pl.ds(my_rows, share), pl.ds(begin, end - begin)]
        gathers = [small_copy(mine, mine, {"pair": lane_at(k)}) for k in range(1, lanes)]
        for copy in gathers:
            copy.start()
        return gathers

    def send_cameras(it, sums, back_copy):
        back_copy.wait_recv()
        sums = jnp.concatenate([sums[0:EDGE, :] + back_c[it, 1], sums[EDGE:own, :]], 0)
        if own < 128:
            sums = jnp.concatenate([sums, jnp.zeros((128 - own, 128), F32)], 0)
        part_c[it, lane] = jnp.transpose(sums)[0:16, :]
        copies = [small_copy(part_c.at[it, lane], part_c.at[it, lane], {"pair": lane_at(k)}) for k in range(1, lanes)]
        for copy in copies:
            copy.start()
        return copies

    def update_cameras(it, copies):
        for copy in copies:
            copy.wait_recv()
        q, turn, turn_inverse, near_focal = camera_parts()
        found = part_c[it, 0]
        for k in range(1, lanes):
            found = found + part_c[it, k]
        across_sum = [found[4 * k : 4 * k + 1, :] * near_focal for k in range(3)]
        down_sum = [found[4 * k + 1 : 4 * k + 2, :] * near_focal for k in range(3)]
        g_turn = [[across_sum[k], down_sum[k], found[4 * k + 2 : 4 * k + 3, :]] for k in range(3)]
        g_cam = rotation_pull(q, turn, turn_inverse, g_turn)
        for k in range(3):
            g_cam.append(found[4 * k + 3 : 4 * k + 4, :])
        g_cam.append(-sum(turn[k][0] * across_sum[k] + turn[k][1] * down_sum[k] for k in range(3)))
        for k in range(8):
            row = slice(k, k + 1)
            cam[row, :], cmean[row, :], csq[row, :] = adam(cam[row, :], g_cam[k], cmean[row, :], csq[row, :], it)

    def send_sums(it):
        second_out[it] = halves(rows_s[pair_lanes : pair_lanes + slots, :])

        def send(j, inner):
            send_row(second_out.at[it], second_in.at[it], 2 + CHUNKS + it, j, behind(j))
            return inner

        lax.fori_loop(1, regions, send, 0)

    def update_pairs(it, with_slots):
        wait_rows(recv_sem, 2 + CHUNKS + it, regions - 1)
        seconds = jnp.concatenate([from_halves(second_in[it]), rows_s[near_at:pair_lanes, :]], 0)
        of_pairs = dot_exact(back_hot[...], seconds)
        found = [of_pairs[0:near_at] + rows_s[0:near_at, :], of_pairs[near_at:pair_lanes]]
        if with_slots:
            wait_rows(recv_sem, 1 + CHUNKS, regions - 1)
            found.append(from_halves(first_in[...]) + rows_s[pair_lanes : pair_lanes + slots, :])
            if slots < total_rows - pair_lanes:
                found.append(jnp.zeros((total_rows - pair_lanes - slots, 128), F32))
        found = jnp.transpose(jnp.concatenate(found, 0))
        lanes_used = slice(0, total_rows if with_slots else pair_lanes)
        m = [[found[COEFS + 4 * k + j : COEFS + 4 * k + j + 1, :] for j in range(3)] for k in range(3)]
        v = [found[4 * k + 3 : 4 * k + 4, :] for k in range(3)]
        p = [pose[k : k + 1, lanes_used] for k in range(4)]
        bend, bend_inverse = rotation_rows(*p)
        scale = jnp.exp(pose[7:8, lanes_used])
        g_turn = [[-(scale * m[k][j]) for j in range(3)] for k in range(3)]
        g_pose = rotation_pull(p, bend, bend_inverse, g_turn)
        g_scale = sum(bend[k][j] * g_turn[k][j] for k in range(3) for j in range(3))
        for k in range(3):
            g_move = -(scale * v[k])
            g_scale = g_scale + pose[4 + k : 5 + k, lanes_used] * g_move
            g_pose.append(g_move)
        g_pose.append(g_scale)
        for k in range(8):
            row = (slice(k, k + 1), lanes_used)
            pose[row], pmean[row], psq[row] = adam(pose[row], g_pose[k], pmean[row], psq[row], it)

    near_side = slice(0, pair_lanes)
    far_side = slice(pair_lanes, total_rows)
    sent = []


    def send_chunk(h):
        def send(j, carry):
            at = pl.ds(pl.multiple_of((j - 1) * MSG + h * chunk, 8), chunk)
            pltpu.make_async_remote_copy(
                src_ref=bulk_out.at[at],
                dst_ref=bulk_in.at[at],
                send_sem=send_sem.at[1 + h],
                recv_sem=recv_sem.at[1 + h],
                device_id={"region": ahead(j)},
            ).start()
            return carry

        lax.fori_loop(1, regions, send, 0)

    edges = [camera_coefs(0), depths(0)]
    pl.semaphore_wait(barrier, regions - 1 + lanes - 1 + jnp.where(lane == 0, 0, 1))

    def send_small(j, carry):
        send_row(small_out, small_in, 0, j, ahead(j))
        return carry

    lax.fori_loop(1, regions, send_small, 0)
    chunk = MSG // CHUNKS
    for copy in edges:
        copy.start()
    sent += edges
    for h in range(CHUNKS - 1):
        send_chunk(h)
    for m in range(3):
        xs[m, 0:pairs, :] = points[m].astype(F32)
    cw[0:pairs, :] = conf[:, 0, :].astype(F32) * weight_column[0:pairs]
    hot = one_hots(jnp.concatenate([as_column(firsts)[0:near_at], near], 0), pair_lanes)
    gather_hot[0:pair_lanes, :] = hot.astype(BF16)
    scatter_hot[:, 0:pair_lanes] = jnp.transpose(hot[:, 0:128]).astype(BF16)
    place_ids = lax.broadcasted_iota(jnp.int32, back_hot.shape, 1).astype(F32)
    back_hot[...] = jnp.where(as_column(place) == place_ids, 1.0, 0.0).astype(BF16)

    down_step = 8.0 * (128 // ANCH_W)
    row_ids = lax.broadcasted_iota(jnp.int32, (128, 128), 0)
    anchor = lax.broadcasted_iota(jnp.int32, (128, 128), 1)
    anchor_row = lax.div(anchor, jnp.full_like(anchor, ANCH_W))
    across = (8 * (anchor - anchor_row * ANCH_W) + 4 - 4 * ANCH_W).astype(F32)
    downward = (8 * anchor_row + 4 - 4 * ANCH_H).astype(F32)
    kind = lax.rem(row_ids, jnp.full_like(row_ids, COEFS))
    kind = jnp.where(row_ids < 3 * COEFS, kind, -1)
    for k in range(3):
        ray = jnp.where(kind == 4 * k, across, jnp.where(kind == 4 * k + 1, downward, jnp.where(kind == 4 * k + 2, 1.0, 0.0)))
        step = jnp.where(kind == 4 * k + 1, down_step, 0.0)
        move = jnp.where(kind == 4 * k + 3, 1.0, 0.0)
        for b, value in ((k, ray), (3 + k, step), (6 + k, move)):
            camera_ones[:, 128 * b : 128 * b + 128] = value.astype(BF16)
        for j in range(4):
            b = 4 * k + j
            pose_ones[:, 128 * b : 128 * b + 128] = jnp.where(kind == b, 1.0, 0.0).astype(BF16)
    across = across[0:8, :]
    downward = downward[0:8, :]

    rows_g[...] = jnp.zeros_like(rows_g)
    rows_s[...] = jnp.zeros_like(rows_s)
    gather_depths(0, near_at)
    gather_cameras(0, near_at)
    pair_rows(False)
    groups(0, near_at)
    first_out[...] = halves(dot_exact(pick_hot[0:slots, :], rows_s[0:pair_lanes, :]))

    def send_first(j, inner):
        send_row(first_out, first_in, 1 + CHUNKS, j, ahead(j))
        return inner

    lax.fori_loop(1, regions, send_first, 0)
    edge_rows(0, edges)
    for part, value in scatter(near_side, 0, keys):
        grad_d[:, part] = value
    grad_s[...] = dot_exact(scatter_hot[0:keys, near_side], rows_s[near_side, :])
    back, edge_sem = send_edges_back(0)
    sent += back
    send_chunk(CHUNKS - 1)
    wait_rows(recv_sem, 0, regions - 1)
    named = from_halves(small_in[...])
    hot = one_hots(named[:, 24:25], slots)
    gather_hot[pair_lanes : pair_lanes + slots, :] = hot.astype(BF16)
    if slots < 128:
        hot = jnp.concatenate([hot, jnp.zeros((128 - slots, hot.shape[1]), F32)], 0)
        named = jnp.concatenate([named, jnp.ones((128 - slots, 128), F32)], 0)
    scatter_hot[:, far_side] = jnp.transpose(hot[:, 0:128]).astype(BF16)
    named = jnp.transpose(named)
    pose[:, far_side] = named[0:8, :]
    pmean[:, far_side] = named[8:16, :]
    psq[:, far_side] = named[16:24, :]
    pose_rows(pair_lanes, pair_coefs()[pair_lanes : pair_lanes + slots])
    gather_cameras(pair_lanes, slots)
    gather_depths(pair_lanes, slots)
    tiles = TILES // CHUNKS
    for h in range(CHUNKS):
        wait_rows(recv_sem, 1 + h, chunk * (regions - 1))
        begin, end = 128 * tiles * h, 128 * tiles * (h + 1)
        for c in range(CAP):
            for g in range(regions // 8):
                at = pair_lanes + c * regions + 8 * g
                for t in range(tiles * h, tiles * (h + 1)):
                    for m in range(MAPS):
                        source = MSG * 8 * g + CAP * MAPS * t + MAPS * c + m
                        value = bulk_in[pl.ds(source, 8, stride=MSG), :]
                        if m < 3:
                            xs[m, at : at + 8, 128 * t : 128 * t + 128] = value
                        else:
                            cw[at : at + 8, 128 * t : 128 * t + 128] = value
        groups(pair_lanes, slots, tiles * h, tiles * (h + 1))
        for part, value in scatter(far_side, 0, own, begin, end):
            grad_d[0:own, part] = grad_d[0:own, part] + value
    shares = send_shares(0, 0, ANCH)
    sums = grad_s[0:own, :] + dot_exact(scatter_hot[0:own, far_side], rows_s[far_side, :])
    cameras = send_cameras(0, sums, back[1])
    sent += cameras
    send_sums(0)
    take_edges(0, edge_sem)
    gathers = update_depths(0, 0, ANCH, shares)
    update_cameras(0, cameras)
    edges = [camera_coefs(1)]
    edges[0].start()
    gather_cameras(0, near_at)
    gather_cameras(pair_lanes, slots)
    update_pairs(0, True)
    pair_rows(True)

    for copy in gathers:
        copy.wait_recv()
    sent += gathers
    edges.append(depths(1))
    sent += edges
    gather_depths(0, near_at)
    gather_depths(pair_lanes, slots)
    groups(0, near_at)
    groups(pair_lanes, slots)
    edge_rows(1, edges)
    for copy in shares:
        copy.wait_send()
    rows = slice(0, total_rows)
    for part, value in scatter(rows, 0, keys):
        grad_d[:, part] = value
    shares = send_shares(1, 0, ANCH)
    grad_s[...] = dot_exact(scatter_hot[0:keys, rows], rows_s[rows, :])
    back, edge_sem = send_edges_back(1)
    send_sums(1)
    cameras = send_cameras(1, grad_s[0:own, :], back[1])
    take_edges(1, edge_sem)
    gathers = update_depths(1, 0, ANCH, shares)
    sent += shares + back + cameras
    update_cameras(1, cameras)
    update_pairs(1, False)

    wait_rows(send_sem, 0, regions - 1)
    for h in range(CHUNKS):
        wait_rows(send_sem, 1 + h, chunk * (regions - 1))
    for n in range(1 + ITERS):
        wait_rows(send_sem, 1 + CHUNKS + n, regions - 1)
    for copy in sent:
        copy.wait_send()
    cam_in[...] = cam[:, 0:own]
    pose_in[...] = pose[:, 0:pairs]
    pmean_in[...] = pmean[:, 0:pairs]
    psq_in[...] = psq[:, 0:pairs]
    for n, src in enumerate((cmean, csq)):
        value = src[:, 0:share]
        for k in range(1, lanes):
            value = jnp.where(lane == k, src[:, k * share : (k + 1) * share], value)
        moments[n] = value
    stores = [
        pltpu.make_async_copy(src, dst, load_sem.at[n])
        for n, (src, dst) in enumerate(
            (
                (logd.at[ITERS], logd_out), (cam_in, cam_out), (pose_in, pose_out), (dmean, dmean_out), (dsq, dsq_out),
                (moments.at[0], cmean_out), (moments.at[1], csq_out), (pmean_in, pmean_out), (psq_in, psq_out),
            )
        )
    ]
    for store in stores[1:]:
        store.start()
    for copy in gathers:
        copy.wait()
    stores[0].start()
    for store in stores:
        store.wait()


def deliver(*refs):
    sources, results, held, sems = refs[0:9], refs[9:18], refs[18:27], refs[27]
    for bring in (True, False):
        copies = [
            pltpu.make_async_copy(sources[n] if bring else held[n], held[n] if bring else results[n], sems.at[n])
            for n in range(9)
        ]
        for copy in copies:
            copy.start()
        for copy in copies:
            copy.wait()


def shards(
    log_depth, cameras, pair_pose, depth_mean, depth_square, camera_mean, camera_square, pose_mean, pose_square,
    pointmaps, confidence, pair_images, pair_flag,
):
    regions = lax.axis_size("region")
    lanes = lax.axis_size("pair")
    own = log_depth.shape[0]
    pairs = pair_pose.shape[0]
    share = own // lanes
    slots = CAP * regions
    nearby = pairs - CAP * (regions - 1)
    pair_lanes = rounded(pairs, 128)
    total_rows = pair_lanes + rounded(slots, 128)
    keys = own + 16
    key_lanes = rounded(3 * keys, 128)
    in_hbm = pl.BlockSpec(memory_space=pltpu.HBM)

    def vmem(*shape, dtype=F32):
        return pltpu.VMEM(shape, dtype)

    def out(*shape):
        return jax.ShapeDtypeStruct(shape, F32)

    shapes = (
        out(own, ANCH), out(8, own), out(8, pairs), out(share, ANCH), out(share, ANCH),
        out(8, share), out(8, share), out(8, pairs), out(8, pairs),
    )
    results = pl.pallas_call(
        functools.partial(kernel, regions, lanes, own, pairs),
        out_shape=shapes,
        in_specs=[in_hbm] * 13,
        out_specs=(in_hbm,) * 9,
        scratch_shapes=[
            vmem(8, own), vmem(8, own), vmem(8, own), vmem(8, pairs), vmem(8, pairs), vmem(8, pairs),
            vmem(2, pairs, dtype=jnp.int32), vmem(1, pairs, dtype=jnp.int32),
            vmem(ITERS + 1, own, ANCH), vmem(share, ANCH), vmem(share, ANCH),
            vmem(8, 128), vmem(8, 128), vmem(8, 128),
            vmem(8, total_rows), vmem(8, total_rows), vmem(8, total_rows),
            vmem(6, pairs, ANCH, dtype=BF16), vmem(pairs, 2, ANCH, dtype=BF16),
            vmem(3, total_rows, ANCH), vmem(total_rows, ANCH),
            vmem(8, pair_lanes, dtype=jnp.int32),
            vmem(slots + nearby, pair_lanes, dtype=BF16), vmem(pair_lanes, slots + nearby, dtype=BF16),
            vmem(total_rows, key_lanes, dtype=BF16), vmem(128, total_rows, dtype=BF16),
            vmem(128, 9 * 128, dtype=BF16), vmem(128, 12 * 128, dtype=BF16),
            vmem(key_lanes, ANCH, dtype=BF16), vmem(key_lanes, 128, dtype=BF16),
            vmem(total_rows, ANCH), vmem(total_rows, 9 * 128), vmem(total_rows, 12 * 128),
            vmem(total_rows, ANCH), vmem(total_rows, 128),
            vmem(128, total_rows), vmem(128, 128), vmem(keys, ANCH), vmem(keys, 128),
            vmem(regions, 128), vmem(regions, 128), vmem(MSG * regions, 128), vmem(MSG * regions, 128),
            vmem(regions, 128), vmem(regions, 128), vmem(ITERS, regions, 128), vmem(ITERS, regions, 128),
            vmem(ITERS, 2, EDGE, ANCH), vmem(ITERS, 2, EDGE, 128),
            vmem(ITERS, EDGE, ANCH), vmem(ITERS, 2, EDGE, 128),
            vmem(ITERS, lanes - 1, share, ANCH), vmem(ITERS, lanes, EDGE, ANCH), vmem(ITERS, lanes, 16, 128), vmem(2, 8, share),
            pltpu.SemaphoreType.DMA((13,)),
            pltpu.SemaphoreType.DMA((2 + CHUNKS + ITERS,)), pltpu.SemaphoreType.DMA((2 + CHUNKS + ITERS,)),
            pltpu.SemaphoreType.DMA((48,)), pltpu.SemaphoreType.DMA((48,)),
        ],
        compiler_params=pltpu.CompilerParams(
            collective_id=0, has_side_effects=True, vmem_limit_bytes=62 * 1024 * 1024
        ),
        name="align",
    )(
        log_depth, cameras.T, pair_pose.T, depth_mean, depth_square, camera_mean.T, camera_square.T,
        pose_mean.T, pose_square.T, pointmaps.transpose(1, 0, 2), confidence,
        pair_images.T, pair_flag.reshape(1, pairs),
    )
    depth, camera, pose, dmean, dsq, cmean, csq, pmean, psq = pl.pallas_call(
        deliver,
        out_shape=shapes,
        in_specs=[in_hbm] * 9,
        out_specs=(in_hbm,) * 9,
        scratch_shapes=[vmem(*shape.shape) for shape in shapes] + [pltpu.SemaphoreType.DMA((9,))],
        compiler_params=pltpu.CompilerParams(vmem_limit_bytes=62 * 1024 * 1024),
        name="deliver",
    )(*results)
    return depth, camera.T, pose.T, dmean, dsq, cmean.T, csq.T, pmean.T, psq.T


def solution(mesh):
    placed = (
        P("region", None),
        P("region", None),
        P(("region", "pair"), None),
        P("region", None),
        P("region", None),
        P("region", None),
        P("region", None),
        P(("region", "pair"), None),
        P(("region", "pair"), None),
        P(("region", "pair"), None, None),
        P(("region", "pair"), None, None),
        P(("region", "pair"), None),
        P(("region", "pair")),
    )
    return jax.shard_map(
        shards,
        mesh=mesh,
        in_specs=placed,
        out_specs=(
            P("region", None),
            P("region", None),
            P(("region", "pair"), None),
            P(("region", "pair"), None),
            P(("region", "pair"), None),
            P(("region", "pair"), None),
            P(("region", "pair"), None),
            P(("region", "pair"), None),
            P(("region", "pair"), None),
        ),
        check_vma=False,
    )
```

```python
import functools

import jax
import jax.numpy as jnp
from jax import lax
from jax.experimental import pallas as pl
from jax.experimental.pallas import tpu as pltpu
from jax.sharding import PartitionSpec as P

ANCH_W = 32
ANCH_H = 24
ANCH = 768
CAP = 2
NEIGHBOURS = 4
ITERS = 2
START = 300

LEARN_RATE = 0.01
BETA_ONE = 0.9
BETA_TWO = 0.999
EPSILON = 1e-08

TILES = ANCH // 128
EDGE = 8
MAPS = 4
MSG = TILES * CAP * MAPS
CHUNKS = 3
COEFS = 16
F32 = jnp.float32
BF16 = jnp.bfloat16


def rounded(value, multiple):
    return -(-value // multiple) * multiple


def split_two(x):
    high = x.astype(BF16)
    return high, (x - high.astype(F32)).astype(BF16)


def split_three(x):
    high = x.astype(BF16)
    rest = x - high.astype(F32)
    middle = rest.astype(BF16)
    return high, middle, (rest - middle.astype(F32)).astype(BF16)


def dot(a, b):
    return jnp.dot(a, b, preferred_element_type=F32)


def dot_exact(one_hot, x):
    high, middle, low = split_three(x)
    return dot(one_hot, high) + (dot(one_hot, middle) + dot(one_hot, low))


def pack_three(x):
    high, middle, low = split_three(x)
    rest = pltpu.roll(middle.astype(F32), COEFS, 1) + pltpu.roll(low.astype(F32), 2 * COEFS, 1)
    return (high.astype(F32) + rest).astype(BF16)


def rotation_rows(w, x, y, z):
    inverse = 1.0 / (w * w + x * x + y * y + z * z)
    matrix = [
        [w * w + x * x - y * y - z * z, 2.0 * (x * y - w * z), 2.0 * (x * z + w * y)],
        [2.0 * (x * y + w * z), w * w - x * x + y * y - z * z, 2.0 * (y * z - w * x)],
        [2.0 * (x * z - w * y), 2.0 * (y * z + w * x), w * w - x * x - y * y + z * z],
    ]
    return [[entry * inverse for entry in line] for line in matrix], inverse


def rotation_pull(q, matrix, inverse, g):
    w, x, y, z = q
    along = sum(g[k][j] * matrix[k][j] for k in range(3) for j in range(3))
    diag = g[0][0] + g[1][1] + g[2][2]
    g_w = w * diag + z * (g[1][0] - g[0][1]) + y * (g[0][2] - g[2][0]) + x * (g[2][1] - g[1][2])
    g_x = (
        x * (g[0][0] - g[1][1] - g[2][2])
        + y * (g[0][1] + g[1][0])
        + z * (g[0][2] + g[2][0])
        + w * (g[2][1] - g[1][2])
    )
    g_y = (
        y * (g[1][1] - g[0][0] - g[2][2])
        + x * (g[0][1] + g[1][0])
        + z * (g[1][2] + g[2][1])
        + w * (g[0][2] - g[2][0])
    )
    g_z = (
        z * (g[2][2] - g[0][0] - g[1][1])
        + x * (g[0][2] + g[2][0])
        + y * (g[1][2] + g[2][1])
        + w * (g[1][0] - g[0][1])
    )
    twice = 2.0 * inverse
    return [twice * (g_w - w * along), twice * (g_x - x * along), twice * (g_y - y * along), twice * (g_z - z * along)]


def adam(param, gradient, mean, square, it):
    fix_one = 1.0 - BETA_ONE ** (START + 1 + it)
    fix_two = 1.0 - BETA_TWO ** (START + 1 + it)
    mean = BETA_ONE * mean + (1.0 - BETA_ONE) * gradient
    square = BETA_TWO * square + (1.0 - BETA_TWO) * gradient * gradient
    param = param - LEARN_RATE * (mean / fix_one) / (jnp.sqrt(square / fix_two) + EPSILON)
    return param, mean, square


def kernel(
    regions, lanes, own, pairs,
    logd_hbm, cam_hbm, pose_hbm, dmean_hbm, dsq_hbm, cmean_hbm, csq_hbm, pmean_hbm, psq_hbm, points_hbm, conf_hbm,
    images_hbm, flag_hbm,
    logd_out, cam_out, pose_out, dmean_out, dsq_out, cmean_out, csq_out, pmean_out, psq_out,
    cam_in, cmean_in, csq_in, pose_in, pmean_in, psq_in, images_in, flag_in,
    logd, dmean, dsq, cam, cmean, csq, pose, pmean, psq, points, conf, xs, cw,
    index_rows, pick_hot, back_hot, gather_hot, scatter_hot, camera_ones, pose_ones,
    table, small_table, rows_d, rows_c, rows_p, rows_g, rows_s, wide, narrow, grad_d, grad_s,
    small_out, small_in, bulk_out, bulk_in, first_out, first_in, second_out, second_in,
    edge_d, edge_c, back_d, back_c, part_d, part_e, part_c, moments,
    load_sem, send_sem, recv_sem, small_send, small_recv,
):
    share = own // lanes
    slots = CAP * regions
    nearby = pairs - CAP * (regions - 1)
    pair_lanes = pose.shape[1] - rounded(slots, 128)
    total_rows = pose.shape[1]
    near_at = pair_lanes - nearby
    keys = own + 16
    region = lax.axis_index("region")
    lane = lax.axis_index("pair")
    my_rows = pl.multiple_of(lane * share, share)

    def ahead(j):
        return lax.rem(region + j, regions)

    def behind(j):
        return lax.rem(region - j + regions, regions)

    def lane_at(k):
        return lax.rem(lane + k, lanes)

    loads = [
        pltpu.make_async_copy(src, dst, load_sem.at[n])
        for n, (src, dst) in enumerate(
            (
                (images_hbm, images_in), (flag_hbm, flag_in), (points_hbm, points), (conf_hbm, conf), (logd_hbm, logd.at[0]),
                (cam_hbm, cam_in), (cmean_hbm, cmean_in), (csq_hbm, csq_in),
                (pose_hbm, pose_in), (pmean_hbm, pmean_in), (psq_hbm, psq_in),
                (dmean_hbm.at[pl.ds(my_rows, share)], dmean), (dsq_hbm.at[pl.ds(my_rows, share)], dsq),
            )
        )
    ]
    for load in loads:
        load.start()

    barrier = pltpu.get_barrier_semaphore()

    def greet(j, carry):
        pl.semaphore_signal(barrier, inc=1, device_id={"region": ahead(j)})
        return carry

    lax.fori_loop(1, regions, greet, 0)
    for k in range(1, lanes):
        pl.semaphore_signal(barrier, inc=1, device_id={"pair": lane_at(k)})


    @pl.when(lane == 0)
    def _():
        for k in range(1, lanes):
            pl.semaphore_signal(barrier, inc=1, device_id={"region": behind(1), "pair": k})

    for load in loads:
        load.wait()

    def as_column(row):
        return jnp.transpose(jnp.broadcast_to(row, (128, row.shape[1])))[:, 0:1]

    lane_ids = lax.broadcasted_iota(jnp.int32, (1, pair_lanes), 1)
    index_rows[...] = jnp.zeros_like(index_rows)
    index_rows[0:2, 0:pairs] = images_in[...]
    index_rows[2:3, 0:pairs] = flag_in[...]
    real = lane_ids < pairs
    seconds = index_rows[1:2, :]
    flags = index_rows[2:3, :]
    remote = jnp.logical_and(flags == 1, real)
    firsts = jnp.where(real, index_rows[0:1, :] - region * own, 0).astype(F32)
    target = lax.div(seconds, jnp.full_like(seconds, own))
    local = seconds - target * own
    offset = target - region
    offset = jnp.where(offset < 0, offset + regions, offset)
    offset = jnp.where(remote, offset, 0).astype(F32)
    near = jnp.where(target == region, local, own + local).astype(F32)
    local = local.astype(F32)
    earlier_ids = lax.broadcasted_iota(jnp.int32, (pair_lanes, pair_lanes), 0)
    later_ids = lax.broadcasted_iota(jnp.int32, (pair_lanes, pair_lanes), 1)
    same = jnp.logical_and(as_column(offset) == offset, earlier_ids < later_ids)
    rank = jnp.sum(jnp.where(same, 1.0, 0.0), axis=0, keepdims=True)
    place = jnp.where(remote, rank * regions + offset - 1.0, slots + rank)
    place = jnp.where(real, place, -1.0)
    place_ids = lax.broadcasted_iota(jnp.int32, pick_hot.shape, 0).astype(F32)
    picked = place_ids == place
    pick_hot[...] = jnp.where(picked, 1.0, 0.0).astype(BF16)
    near = jnp.sum(jnp.where(picked, near, 0.0), axis=1, keepdims=True)[slots : slots + nearby]

    ones = jnp.ones((8, total_rows), F32)
    for padded, values in ((pose, pose_in), (pmean, pmean_in), (psq, psq_in)):
        padded[...] = ones
        padded[:, 0:pairs] = values[...]
    wide[...] = jnp.zeros_like(wide)
    wide[0:8, :] = pose[...]
    wide[8:16, :] = pmean[...]
    wide[16:24, :] = psq[...]
    wide[24:25, 0:pair_lanes] = local
    details = dot_exact(pick_hot[...], jnp.transpose(wide[:, 0:pair_lanes]))[0:slots]
    wide[...] = jnp.zeros_like(wide)

    def halves(values):
        return values[0:regions] + pltpu.roll(values[regions:slots], 64, 1)

    def from_halves(values):
        low = lax.broadcasted_iota(jnp.int32, values.shape, 1) < 64
        return jnp.concatenate([jnp.where(low, values, 0.0), jnp.where(low, pltpu.roll(values, 64, 1), 0.0)], 0)

    small_out[...] = halves(details)
    small_in[regions - 1 : regions, :] = jnp.ones((1, 128), F32)
    bulk_in[MSG * (regions - 1) : MSG * regions, :] = jnp.zeros((MSG, 128), F32)
    first_in[regions - 1 : regions, :] = jnp.zeros((1, 128), F32)
    for it in range(ITERS):
        second_in[it, regions - 1 : regions, :] = jnp.zeros((1, 128), F32)
    weights = 2.0 * (1.0 + flags.astype(F32))
    weights = jnp.where(real, weights, 0.0)
    weight_column = as_column(weights)
    slot_weights = jnp.sum(jnp.where(picked, weights, 0.0), axis=1, keepdims=True)
    xs[...] = jnp.zeros_like(xs)
    cw[...] = jnp.zeros_like(cw)
    for m in range(MAPS):
        source = points[3 + m] if m < 3 else conf[:, 1, :]
        chosen = dot(pick_hot[:, 0:pairs], source)
        if m == 3:
            chosen = chosen * slot_weights
        for c in range(CAP):
            for g in range(regions // 8):
                rows = slice(c * regions + 8 * g, c * regions + 8 * g + 8)
                for t in range(TILES):
                    at = MSG * 8 * g + CAP * MAPS * t + MAPS * c + m
                    bulk_out[pl.ds(at, 8, stride=MSG), :] = chosen[rows, 128 * t : 128 * t + 128]
        if m < 3:
            xs[m, near_at:pair_lanes, :] = chosen[slots : slots + nearby]
        else:
            cw[near_at:pair_lanes, :] = chosen[slots : slots + nearby]

    def send_row(src, dst, which, j, to):
        at = pl.ds(j - 1, 1)
        pltpu.make_async_remote_copy(
            src_ref=src.at[at],
            dst_ref=dst.at[at],
            send_sem=send_sem.at[which],
            recv_sem=recv_sem.at[which],
            device_id={"region": to},
        ).start()

    def wait_rows(sem, which, count):
        whole = bulk_in.at[pl.ds(0, count)]
        pltpu.make_async_copy(whole, whole, sem.at[which]).wait()

    def one_hots(column, count):
        key_ids = lax.broadcasted_iota(jnp.int32, (count, gather_hot.shape[1]), 1)
        for n in (2, 1):
            key_ids = jnp.where(key_ids >= n * keys, jnp.where(key_ids < 3 * keys, key_ids - n * keys, -1), key_ids)
        return jnp.where(column == key_ids.astype(F32), 1.0, 0.0)

    column_ids = lax.broadcasted_iota(jnp.int32, (8, 128), 1)
    for padded, values in ((cam, cam_in), (cmean, cmean_in), (csq, csq_in)):
        padded[...] = jnp.ones((8, 128), F32)
        padded[:, 0:own] = values[...]
    narrow[...] = jnp.zeros_like(narrow)
    table[...] = jnp.zeros_like(table)
    small_table[...] = jnp.zeros_like(small_table)

    counter = iter(range(small_send.shape[0]))

    def small_copy(src, dst, device_id):
        which = next(counter)
        return pltpu.make_async_remote_copy(
            src_ref=src,
            dst_ref=dst,
            send_sem=small_send.at[which],
            recv_sem=small_recv.at[which],
            device_id=device_id,
        )

    def fill(ref, at, values):
        for n, piece in enumerate(split_three(values)):
            ref[n * keys + at : n * keys + at + values.shape[0], 0 : values.shape[1]] = piece

    def gather_depths(at, count, begin=0, end=ANCH):
        for n in range(begin, end, 256):
            rows_d[at : at + count, n : n + 256] = dot(gather_hot[at : at + count, :], table[:, n : n + 256])

    def gather_cameras(at, count):
        values = dot(gather_hot[at : at + count, :], small_table[...])
        rows_c[at : at + count, :] = dot(pack_three(values), camera_ones[...])

    def pose_rows(at, values):
        rows_p[at : at + values.shape[0], :] = dot(pack_three(values), pose_ones[...])

    def group(g, inner, begin=0, end=TILES):
        at = pl.ds(pl.multiple_of(g * 8, 8), 8)

        def block(ref, b):
            return ref[at, 128 * b : 128 * b + 128]

        shift = [[block(rows_p, 4 * k + j) for j in range(4)] for k in range(3)]
        ray = [block(rows_c, k) for k in range(3)]
        if begin > 0:
            ray = [ray[k] + F32(begin) * block(rows_c, 3 + k) for k in range(3)]
        zero = jnp.zeros((8, 128), F32)
        turned = [[zero for j in range(3)] for k in range(3)]
        total = [zero for k in range(3)]
        by_depth = [zero for k in range(3)]
        by_down = [zero for k in range(3)]
        for t in range(begin, end):
            part = slice(128 * t, 128 * t + 128)
            d = rows_d[at, part]
            c = cw[at, part]
            x = [xs[j, at, part] for j in range(3)]
            along = None
            for k in range(3):
                placed = shift[k][0] * x[0] + shift[k][1] * x[1] + (shift[k][2] * x[2] + shift[k][3])
                pull = c * ((d * ray[k] + block(rows_c, 6 + k)) - placed)
                for j in range(3):
                    turned[k][j] = turned[k][j] + pull * x[j]
                total[k] = total[k] + pull
                deep = pull * d
                by_depth[k] = by_depth[k] + deep
                if t > 0:
                    by_down[k] = by_down[k] + F32(t) * deep
                along = deep * ray[k] if along is None else along + deep * ray[k]
                if t < end - 1:
                    ray[k] = ray[k] + block(rows_c, 3 + k)
            rows_g[at, part] = along
        out = zero
        for k in range(3):
            values = [by_depth[k] * across, by_depth[k] * downward + by_down[k] * down_step, by_depth[k], total[k]]
            for j in range(4):
                out = jnp.where(column_ids == 4 * k + j, jnp.sum(values[j], axis=1, keepdims=True), out)
            for j in range(3):
                column = COEFS + 4 * k + j
                out = jnp.where(column_ids == column, jnp.sum(turned[k][j], axis=1, keepdims=True), out)
        rows_s[at, :] = out if begin == 0 else rows_s[at, :] + out
        return inner

    def groups(at, count, begin=0, end=TILES):
        lax.fori_loop(at // 8, (at + count) // 8, functools.partial(group, begin=begin, end=end), 0, unroll=4)

    def scatter(rows, keys_from, keys_to, begin=0, end=ANCH):
        hot = scatter_hot[keys_from:keys_to, rows]
        for n in range(begin, end, 256):
            high, low = split_two(rows_g[rows, n : n + 256])
            yield slice(n, n + 256), dot(hot, high) + dot(hot, low)

    def camera_parts():
        q = [cam[k : k + 1, :] for k in range(4)]
        turn, turn_inverse = rotation_rows(*q)
        return q, turn, turn_inverse, jnp.exp(-cam[7:8, :])

    def camera_coefs(it):
        q, turn, turn_inverse, near_focal = camera_parts()
        for k in range(3):
            narrow[4 * k : 4 * k + 1, :] = turn[k][0] * near_focal
            narrow[4 * k + 1 : 4 * k + 2, :] = turn[k][1] * near_focal
            narrow[4 * k + 2 : 4 * k + 3, :] = turn[k][2]
            narrow[4 * k + 3 : 4 * k + 4, :] = cam[4 + k : 5 + k, :]
        coefs = jnp.transpose(narrow[...])[0:own, :]
        edge_c[it, 0] = coefs[0:EDGE, :]
        fill(small_table, 0, coefs)
        return small_copy(edge_c.at[it, 0], edge_c.at[it, 1], {"region": behind(1)})

    def pair_coefs():
        p = [pose[k : k + 1, :] for k in range(4)]
        bend, bend_inverse = rotation_rows(*p)
        scale = jnp.exp(pose[7:8, :])
        for k in range(3):
            for j in range(3):
                wide[4 * k + j : 4 * k + j + 1, :] = scale * bend[k][j]
            wide[4 * k + 3 : 4 * k + 4, :] = scale * pose[4 + k : 5 + k, :]
        return jnp.transpose(wide[...])

    def pair_rows(with_slots):
        values = pair_coefs()
        near_values = dot_exact(pick_hot[slots : slots + nearby, :], values[0:pair_lanes])
        values = [values[0:near_at], near_values] + ([values[pair_lanes : pair_lanes + slots]] if with_slots else [])
        pose_rows(0, jnp.concatenate(values, 0))

    def depths(it):
        depth = jnp.exp(logd[it])
        edge_d[it, 0] = depth[0:EDGE, :]
        copy = small_copy(edge_d.at[it, 0], edge_d.at[it, 1], {"region": behind(1)})
        if it > 0:
            copy.start()
        fill(table, 0, depth)
        return copy

    def edge_rows(it, copies):
        for copy in copies:
            copy.wait_recv()
        blank = jnp.zeros((8, ANCH), F32)
        fill(table, own, jnp.concatenate([edge_d[it, 1], blank], 0))
        fill(small_table, own, jnp.concatenate([edge_c[it, 1], blank[:, 0:128]], 0))
        gather_depths(near_at, nearby)
        gather_cameras(near_at, nearby)
        groups(near_at, nearby)

    def send_edges_back(it):
        back_d[it] = grad_d[own : own + EDGE, :]
        back_c[it, 0] = grad_s[own : own + EDGE, :]
        which = next(counter)
        to_owner = pltpu.make_async_remote_copy(
            src_ref=back_d.at[it],
            dst_ref=part_e.at[it, lane],
            send_sem=small_send.at[which],
            recv_sem=small_recv.at[which],
            device_id={"region": ahead(1), "pair": 0},
        )
        copies = [to_owner, small_copy(back_c.at[it, 0], back_c.at[it, 1], {"region": ahead(1)})]
        for copy in copies:
            copy.start()
        return copies, which

    def take_edges(it, which):
        @pl.when(lane == 0)
        def _():
            whole = part_e.at[it]
            pltpu.make_async_copy(whole, whole, small_recv.at[which]).wait()
            total = part_e[it, 0]
            for k in range(1, lanes):
                total = total + part_e[it, k]
            grad_d[0:EDGE, :] = grad_d[0:EDGE, :] + total

    def send_shares(it, begin, end):
        copies = []
        for k in range(1, lanes):
            to = lane_at(k)
            rows = pl.ds(pl.multiple_of(to * share, share), share)
            columns = pl.ds(begin, end - begin)
            copies.append(small_copy(grad_d.at[rows, columns], part_d.at[it, k - 1, :, columns], {"pair": to}))
        for copy in copies:
            copy.start()
        return copies

    def update_depths(it, begin, end, copies):
        for copy in copies:
            copy.wait_recv()
        columns = slice(begin, end)
        gradient = grad_d[pl.ds(my_rows, share), columns]
        for k in range(1, lanes):
            gradient = gradient + part_d[it, k - 1, :, columns]
        updated, dmean[:, columns], dsq[:, columns] = adam(
            logd[it, pl.ds(my_rows, share), columns], gradient, dmean[:, columns], dsq[:, columns], it
        )
        logd[it + 1, pl.ds(my_rows, share), columns] = updated
        mine = logd.at[it + 1, pl.ds(my_rows, share), pl.ds(begin, end - begin)]
        gathers = [small_copy(mine, mine, {"pair": lane_at(k)}) for k in range(1, lanes)]
        for copy in gathers:
            copy.start()
        return gathers

    def send_cameras(it, sums, back_copy):
        back_copy.wait_recv()
        sums = jnp.concatenate([sums[0:EDGE, :] + back_c[it, 1], sums[EDGE:own, :]], 0)
        if own < 128:
            sums = jnp.concatenate([sums, jnp.zeros((128 - own, 128), F32)], 0)
        part_c[it, lane] = jnp.transpose(sums)[0:16, :]
        copies = [small_copy(part_c.at[it, lane], part_c.at[it, lane], {"pair": lane_at(k)}) for k in range(1, lanes)]
        for copy in copies:
            copy.start()
        return copies

    def update_cameras(it, copies):
        for copy in copies:
            copy.wait_recv()
        q, turn, turn_inverse, near_focal = camera_parts()
        found = part_c[it, 0]
        for k in range(1, lanes):
            found = found + part_c[it, k]
        across_sum = [found[4 * k : 4 * k + 1, :] * near_focal for k in range(3)]
        down_sum = [found[4 * k + 1 : 4 * k + 2, :] * near_focal for k in range(3)]
        g_turn = [[across_sum[k], down_sum[k], found[4 * k + 2 : 4 * k + 3, :]] for k in range(3)]
        g_cam = rotation_pull(q, turn, turn_inverse, g_turn)
        for k in range(3):
            g_cam.append(found[4 * k + 3 : 4 * k + 4, :])
        g_cam.append(-sum(turn[k][0] * across_sum[k] + turn[k][1] * down_sum[k] for k in range(3)))
        for k in range(8):
            row = slice(k, k + 1)
            cam[row, :], cmean[row, :], csq[row, :] = adam(cam[row, :], g_cam[k], cmean[row, :], csq[row, :], it)

    def send_sums(it):
        second_out[it] = halves(rows_s[pair_lanes : pair_lanes + slots, :])

        def send(j, inner):
            send_row(second_out.at[it], second_in.at[it], 2 + CHUNKS + it, j, behind(j))
            return inner

        lax.fori_loop(1, regions, send, 0)

    def update_pairs(it, with_slots):
        wait_rows(recv_sem, 2 + CHUNKS + it, regions - 1)
        seconds = jnp.concatenate([from_halves(second_in[it]), rows_s[near_at:pair_lanes, :]], 0)
        of_pairs = dot_exact(back_hot[...], seconds)
        found = [of_pairs[0:near_at] + rows_s[0:near_at, :], of_pairs[near_at:pair_lanes]]
        if with_slots:
            wait_rows(recv_sem, 1 + CHUNKS, regions - 1)
            found.append(from_halves(first_in[...]) + rows_s[pair_lanes : pair_lanes + slots, :])
            if slots < total_rows - pair_lanes:
                found.append(jnp.zeros((total_rows - pair_lanes - slots, 128), F32))
        found = jnp.transpose(jnp.concatenate(found, 0))
        lanes_used = slice(0, total_rows if with_slots else pair_lanes)
        m = [[found[COEFS + 4 * k + j : COEFS + 4 * k + j + 1, :] for j in range(3)] for k in range(3)]
        v = [found[4 * k + 3 : 4 * k + 4, :] for k in range(3)]
        p = [pose[k : k + 1, lanes_used] for k in range(4)]
        bend, bend_inverse = rotation_rows(*p)
        scale = jnp.exp(pose[7:8, lanes_used])
        g_turn = [[-(scale * m[k][j]) for j in range(3)] for k in range(3)]
        g_pose = rotation_pull(p, bend, bend_inverse, g_turn)
        g_scale = sum(bend[k][j] * g_turn[k][j] for k in range(3) for j in range(3))
        for k in range(3):
            g_move = -(scale * v[k])
            g_scale = g_scale + pose[4 + k : 5 + k, lanes_used] * g_move
            g_pose.append(g_move)
        g_pose.append(g_scale)
        for k in range(8):
            row = (slice(k, k + 1), lanes_used)
            pose[row], pmean[row], psq[row] = adam(pose[row], g_pose[k], pmean[row], psq[row], it)

    near_side = slice(0, pair_lanes)
    far_side = slice(pair_lanes, total_rows)
    sent = []


    def send_chunk(h):
        def send(j, carry):
            at = pl.ds(pl.multiple_of((j - 1) * MSG + h * chunk, 8), chunk)
            pltpu.make_async_remote_copy(
                src_ref=bulk_out.at[at],
                dst_ref=bulk_in.at[at],
                send_sem=send_sem.at[1 + h],
                recv_sem=recv_sem.at[1 + h],
                device_id={"region": ahead(j)},
            ).start()
            return carry

        lax.fori_loop(1, regions, send, 0)

    edges = [camera_coefs(0), depths(0)]
    pl.semaphore_wait(barrier, regions - 1 + lanes - 1 + jnp.where(lane == 0, 0, 1))

    def send_small(j, carry):
        send_row(small_out, small_in, 0, j, ahead(j))
        return carry

    lax.fori_loop(1, regions, send_small, 0)
    chunk = MSG // CHUNKS
    for copy in edges:
        copy.start()
    sent += edges
    for h in range(CHUNKS - 1):
        send_chunk(h)
    for m in range(3):
        xs[m, 0:pairs, :] = points[m].astype(F32)
    cw[0:pairs, :] = conf[:, 0, :].astype(F32) * weight_column[0:pairs]
    hot = one_hots(jnp.concatenate([as_column(firsts)[0:near_at], near], 0), pair_lanes)
    gather_hot[0:pair_lanes, :] = hot.astype(BF16)
    scatter_hot[:, 0:pair_lanes] = jnp.transpose(hot[:, 0:128]).astype(BF16)
    place_ids = lax.broadcasted_iota(jnp.int32, back_hot.shape, 1).astype(F32)
    back_hot[...] = jnp.where(as_column(place) == place_ids, 1.0, 0.0).astype(BF16)

    down_step = 8.0 * (128 // ANCH_W)
    row_ids = lax.broadcasted_iota(jnp.int32, (128, 128), 0)
    anchor = lax.broadcasted_iota(jnp.int32, (128, 128), 1)
    anchor_row = lax.div(anchor, jnp.full_like(anchor, ANCH_W))
    across = (8 * (anchor - anchor_row * ANCH_W) + 4 - 4 * ANCH_W).astype(F32)
    downward = (8 * anchor_row + 4 - 4 * ANCH_H).astype(F32)
    kind = lax.rem(row_ids, jnp.full_like(row_ids, COEFS))
    kind = jnp.where(row_ids < 3 * COEFS, kind, -1)
    for k in range(3):
        ray = jnp.where(kind == 4 * k, across, jnp.where(kind == 4 * k + 1, downward, jnp.where(kind == 4 * k + 2, 1.0, 0.0)))
        step = jnp.where(kind == 4 * k + 1, down_step, 0.0)
        move = jnp.where(kind == 4 * k + 3, 1.0, 0.0)
        for b, value in ((k, ray), (3 + k, step), (6 + k, move)):
            camera_ones[:, 128 * b : 128 * b + 128] = value.astype(BF16)
        for j in range(4):
            b = 4 * k + j
            pose_ones[:, 128 * b : 128 * b + 128] = jnp.where(kind == b, 1.0, 0.0).astype(BF16)
    across = across[0:8, :]
    downward = downward[0:8, :]

    rows_g[...] = jnp.zeros_like(rows_g)
    rows_s[...] = jnp.zeros_like(rows_s)
    gather_depths(0, near_at)
    gather_cameras(0, near_at)
    pair_rows(False)
    groups(0, near_at)
    first_out[...] = halves(dot_exact(pick_hot[0:slots, :], rows_s[0:pair_lanes, :]))

    def send_first(j, inner):
        send_row(first_out, first_in, 1 + CHUNKS, j, ahead(j))
        return inner

    lax.fori_loop(1, regions, send_first, 0)
    edge_rows(0, edges)
    for part, value in scatter(near_side, 0, keys):
        grad_d[:, part] = value
    grad_s[...] = dot_exact(scatter_hot[0:keys, near_side], rows_s[near_side, :])
    back, edge_sem = send_edges_back(0)
    sent += back
    send_chunk(CHUNKS - 1)
    wait_rows(recv_sem, 0, regions - 1)
    named = from_halves(small_in[...])
    hot = one_hots(named[:, 24:25], slots)
    gather_hot[pair_lanes : pair_lanes + slots, :] = hot.astype(BF16)
    if slots < 128:
        hot = jnp.concatenate([hot, jnp.zeros((128 - slots, hot.shape[1]), F32)], 0)
        named = jnp.concatenate([named, jnp.ones((128 - slots, 128), F32)], 0)
    scatter_hot[:, far_side] = jnp.transpose(hot[:, 0:128]).astype(BF16)
    named = jnp.transpose(named)
    pose[:, far_side] = named[0:8, :]
    pmean[:, far_side] = named[8:16, :]
    psq[:, far_side] = named[16:24, :]
    pose_rows(pair_lanes, pair_coefs()[pair_lanes : pair_lanes + slots])
    gather_cameras(pair_lanes, slots)
    gather_depths(pair_lanes, slots)
    tiles = TILES // CHUNKS
    for h in range(CHUNKS):
        if h == CHUNKS - 1:
            early = send_shares(0, 0, 128 * tiles * h)
        wait_rows(recv_sem, 1 + h, chunk * (regions - 1))
        begin, end = 128 * tiles * h, 128 * tiles * (h + 1)
        for c in range(CAP):
            for g in range(regions // 8):
                at = pair_lanes + c * regions + 8 * g
                for t in range(tiles * h, tiles * (h + 1)):
                    for m in range(MAPS):
                        source = MSG * 8 * g + CAP * MAPS * t + MAPS * c + m
                        value = bulk_in[pl.ds(source, 8, stride=MSG), :]
                        if m < 3:
                            xs[m, at : at + 8, 128 * t : 128 * t + 128] = value
                        else:
                            cw[at : at + 8, 128 * t : 128 * t + 128] = value
        groups(pair_lanes, slots, tiles * h, tiles * (h + 1))
        for part, value in scatter(far_side, 0, own, begin, end):
            grad_d[0:own, part] = grad_d[0:own, part] + value
    shares = send_shares(0, begin, ANCH)
    sums = grad_s[0:own, :] + dot_exact(scatter_hot[0:own, far_side], rows_s[far_side, :])
    cameras = send_cameras(0, sums, back[1])
    sent += cameras
    send_sums(0)
    take_edges(0, edge_sem)
    gathers = update_depths(0, 0, begin, early)
    gathers += update_depths(0, begin, ANCH, shares)
    update_cameras(0, cameras)
    edges = [camera_coefs(1)]
    edges[0].start()
    gather_cameras(0, near_at)
    gather_cameras(pair_lanes, slots)
    update_pairs(0, True)
    pair_rows(True)

    for copy in gathers:
        copy.wait_recv()
    sent += gathers
    edges.append(depths(1))
    sent += edges
    gather_depths(0, near_at)
    gather_depths(pair_lanes, slots)
    groups(0, near_at)
    groups(pair_lanes, slots)
    edge_rows(1, edges)
    for copy in early + shares:
        copy.wait_send()
    rows = slice(0, total_rows)
    shares = []
    for part, value in scatter(rows, 0, keys):
        grad_d[:, part] = value
        shares.append((part.start, part.stop, send_shares(1, part.start, part.stop)))
    grad_s[...] = dot_exact(scatter_hot[0:keys, rows], rows_s[rows, :])
    back, edge_sem = send_edges_back(1)
    send_sums(1)
    cameras = send_cameras(1, grad_s[0:own, :], back[1])
    take_edges(1, edge_sem)
    gathers = []
    for share_part in shares:
        gathers += update_depths(1, *share_part)
        sent += share_part[2]
    sent += back + cameras
    update_cameras(1, cameras)
    update_pairs(1, False)

    wait_rows(send_sem, 0, regions - 1)
    for h in range(CHUNKS):
        wait_rows(send_sem, 1 + h, chunk * (regions - 1))
    for n in range(1 + ITERS):
        wait_rows(send_sem, 1 + CHUNKS + n, regions - 1)
    for copy in sent:
        copy.wait_send()
    cam_in[...] = cam[:, 0:own]
    pose_in[...] = pose[:, 0:pairs]
    pmean_in[...] = pmean[:, 0:pairs]
    psq_in[...] = psq[:, 0:pairs]
    for n, src in enumerate((cmean, csq)):
        value = src[:, 0:share]
        for k in range(1, lanes):
            value = jnp.where(lane == k, src[:, k * share : (k + 1) * share], value)
        moments[n] = value
    stores = [
        pltpu.make_async_copy(src, dst, load_sem.at[n])
        for n, (src, dst) in enumerate(
            (
                (logd.at[ITERS], logd_out), (cam_in, cam_out), (pose_in, pose_out), (dmean, dmean_out), (dsq, dsq_out),
                (moments.at[0], cmean_out), (moments.at[1], csq_out), (pmean_in, pmean_out), (psq_in, psq_out),
            )
        )
    ]
    for store in stores[1:]:
        store.start()
    for copy in gathers:
        copy.wait()
    stores[0].start()
    for store in stores:
        store.wait()


def deliver(*refs):
    sources, results, held, sems = refs[0:9], refs[9:18], refs[18:27], refs[27]
    for bring in (True, False):
        copies = [
            pltpu.make_async_copy(sources[n] if bring else held[n], held[n] if bring else results[n], sems.at[n])
            for n in range(9)
        ]
        for copy in copies:
            copy.start()
        for copy in copies:
            copy.wait()


def shards(
    log_depth, cameras, pair_pose, depth_mean, depth_square, camera_mean, camera_square, pose_mean, pose_square,
    pointmaps, confidence, pair_images, pair_flag,
):
    regions = lax.axis_size("region")
    lanes = lax.axis_size("pair")
    own = log_depth.shape[0]
    pairs = pair_pose.shape[0]
    share = own // lanes
    slots = CAP * regions
    nearby = pairs - CAP * (regions - 1)
    pair_lanes = rounded(pairs, 128)
    total_rows = pair_lanes + rounded(slots, 128)
    keys = own + 16
    key_lanes = rounded(3 * keys, 128)
    in_hbm = pl.BlockSpec(memory_space=pltpu.HBM)

    def vmem(*shape, dtype=F32):
        return pltpu.VMEM(shape, dtype)

    def out(*shape):
        return jax.ShapeDtypeStruct(shape, F32)

    shapes = (
        out(own, ANCH), out(8, own), out(8, pairs), out(share, ANCH), out(share, ANCH),
        out(8, share), out(8, share), out(8, pairs), out(8, pairs),
    )
    results = pl.pallas_call(
        functools.partial(kernel, regions, lanes, own, pairs),
        out_shape=shapes,
        in_specs=[in_hbm] * 13,
        out_specs=(in_hbm,) * 9,
        scratch_shapes=[
            vmem(8, own), vmem(8, own), vmem(8, own), vmem(8, pairs), vmem(8, pairs), vmem(8, pairs),
            vmem(2, pairs, dtype=jnp.int32), vmem(1, pairs, dtype=jnp.int32),
            vmem(ITERS + 1, own, ANCH), vmem(share, ANCH), vmem(share, ANCH),
            vmem(8, 128), vmem(8, 128), vmem(8, 128),
            vmem(8, total_rows), vmem(8, total_rows), vmem(8, total_rows),
            vmem(6, pairs, ANCH, dtype=BF16), vmem(pairs, 2, ANCH, dtype=BF16),
            vmem(3, total_rows, ANCH), vmem(total_rows, ANCH),
            vmem(8, pair_lanes, dtype=jnp.int32),
            vmem(slots + nearby, pair_lanes, dtype=BF16), vmem(pair_lanes, slots + nearby, dtype=BF16),
            vmem(total_rows, key_lanes, dtype=BF16), vmem(128, total_rows, dtype=BF16),
            vmem(128, 9 * 128, dtype=BF16), vmem(128, 12 * 128, dtype=BF16),
            vmem(key_lanes, ANCH, dtype=BF16), vmem(key_lanes, 128, dtype=BF16),
            vmem(total_rows, ANCH), vmem(total_rows, 9 * 128), vmem(total_rows, 12 * 128),
            vmem(total_rows, ANCH), vmem(total_rows, 128),
            vmem(128, total_rows), vmem(128, 128), vmem(keys, ANCH), vmem(keys, 128),
            vmem(regions, 128), vmem(regions, 128), vmem(MSG * regions, 128), vmem(MSG * regions, 128),
            vmem(regions, 128), vmem(regions, 128), vmem(ITERS, regions, 128), vmem(ITERS, regions, 128),
            vmem(ITERS, 2, EDGE, ANCH), vmem(ITERS, 2, EDGE, 128),
            vmem(ITERS, EDGE, ANCH), vmem(ITERS, 2, EDGE, 128),
            vmem(ITERS, lanes - 1, share, ANCH), vmem(ITERS, lanes, EDGE, ANCH), vmem(ITERS, lanes, 16, 128), vmem(2, 8, share),
            pltpu.SemaphoreType.DMA((13,)),
            pltpu.SemaphoreType.DMA((2 + CHUNKS + ITERS,)), pltpu.SemaphoreType.DMA((2 + CHUNKS + ITERS,)),
            pltpu.SemaphoreType.DMA((64,)), pltpu.SemaphoreType.DMA((64,)),
        ],
        compiler_params=pltpu.CompilerParams(
            collective_id=0, has_side_effects=True, vmem_limit_bytes=62 * 1024 * 1024
        ),
        name="align",
    )(
        log_depth, cameras.T, pair_pose.T, depth_mean, depth_square, camera_mean.T, camera_square.T,
        pose_mean.T, pose_square.T, pointmaps.transpose(1, 0, 2), confidence,
        pair_images.T, pair_flag.reshape(1, pairs),
    )
    depth, camera, pose, dmean, dsq, cmean, csq, pmean, psq = pl.pallas_call(
        deliver,
        out_shape=shapes,
        in_specs=[in_hbm] * 9,
        out_specs=(in_hbm,) * 9,
        scratch_shapes=[vmem(*shape.shape) for shape in shapes] + [pltpu.SemaphoreType.DMA((9,))],
        compiler_params=pltpu.CompilerParams(vmem_limit_bytes=62 * 1024 * 1024),
        name="deliver",
    )(*results)
    return depth, camera.T, pose.T, dmean, dsq, cmean.T, csq.T, pmean.T, psq.T


def solution(mesh):
    placed = (
        P("region", None),
        P("region", None),
        P(("region", "pair"), None),
        P("region", None),
        P("region", None),
        P("region", None),
        P("region", None),
        P(("region", "pair"), None),
        P(("region", "pair"), None),
        P(("region", "pair"), None, None),
        P(("region", "pair"), None, None),
        P(("region", "pair"), None),
        P(("region", "pair")),
    )
    return jax.shard_map(
        shards,
        mesh=mesh,
        in_specs=placed,
        out_specs=(
            P("region", None),
            P("region", None),
            P(("region", "pair"), None),
            P(("region", "pair"), None),
            P(("region", "pair"), None),
            P(("region", "pair"), None),
            P(("region", "pair"), None),
            P(("region", "pair"), None),
            P(("region", "pair"), None),
        ),
        check_vma=False,
    )
```
